32 devices in a mesh: ctx: 8 (over z, core), fsdp: 4 (over y, x).
Axes of the slice: x: 2, y: 2, z: 4, core: 2. Of those that a mesh axis runs over, the one named last changes fastest.
Arguments:
- inputs: bfloat16 [2, 4, 2048, 1024], P(None, 'fsdp', 'ctx'), may hold values from -6 to 6
- block_slots: int32 [2, 4, 16], P(None, 'fsdp'), may hold values from 0 to 15, as said below
- doc_starts: int32 [2, 4, 4], P(None, 'fsdp'), may hold values from 0 to 2047, as said below
- mem_index: int32 [2, 4, 2048, 8, 32], P(None, 'fsdp', 'ctx'), may hold values from 0 to 2047
- mem_keys: bfloat16 [4, 2048, 1024], P('fsdp', 'ctx'), may hold values from -8 to 8
- mem_values: bfloat16 [4, 2048, 1024], P('fsdp', 'ctx'), may hold values from -6 to 6
- out_grad: bfloat16 [2, 4, 2048, 1024], P(None, 'fsdp', 'ctx'), may hold values from -6 to 6
- local_gain_in: bfloat16 [1024], P('fsdp'), may hold values from 0.5 to 1.5
- local_bias_in: bfloat16 [1024], P('fsdp'), may hold values from -1.25 to 1.25
- local_w_qkv: bfloat16 [1024, 3072], P('fsdp'), may hold values from -0.1875 to 0.1875
- local_rel_bias: bfloat16 [8, 32], P('fsdp'), may hold values from -3 to 3
- local_w_out: bfloat16 [1024, 1024], P('fsdp'), may hold values from -0.75 to 0.75
- local_gain_mid: bfloat16 [1024], P('fsdp'), may hold values from 0.5 to 1.5
- local_bias_mid: bfloat16 [1024], P('fsdp'), may hold values from -1.25 to 1.25
- local_w_in: bfloat16 [1024, 4096], P('fsdp'), may hold values from -0.1875 to 0.1875
- local_w_down: bfloat16 [4096, 1024], P('fsdp'), may hold values from -0.09375 to 0.09375
- recall_gain_in: bfloat16 [1024], P('fsdp'), may hold values from 0.5 to 1.5
- recall_bias_in: bfloat16 [1024], P('fsdp'), may hold values from -1.25 to 1.25
- recall_w_qkv: bfloat16 [1024, 3072], P('fsdp'), may hold values from -0.1875 to 0.1875
- recall_rel_bias: bfloat16 [8, 32], P('fsdp'), may hold values from -3 to 3
- recall_w_out: bfloat16 [1024, 1024], P('fsdp'), may hold values from -0.75 to 0.75
- recall_gain_mid: bfloat16 [1024], P('fsdp'), may hold values from 0.5 to 1.5
- recall_bias_mid: bfloat16 [1024], P('fsdp'), may hold values from -1.25 to 1.25
- recall_w_in: bfloat16 [1024, 4096], P('fsdp'), may hold values from -0.1875 to 0.1875
- recall_w_down: bfloat16 [4096, 1024], P('fsdp'), may hold values from -0.09375 to 0.09375
- recall_gate: bfloat16 [8], P('fsdp'), may hold values from -8 to 8
Outputs:
- outputs: bfloat16 [2, 4, 2048, 1024], P(None, 'fsdp', 'ctx')
- input_grad: float32 [2, 4, 2048, 1024], P(None, 'fsdp', 'ctx')
- grad_local_gain_in: float32 [1024], P('fsdp')
- grad_local_bias_in: float32 [1024], P('fsdp')
- grad_local_w_qkv: float32 [1024, 3072], P('fsdp')
- grad_local_rel_bias: float32 [8, 32], P('fsdp')
- grad_local_w_out: float32 [1024, 1024], P('fsdp')
- grad_local_gain_mid: float32 [1024], P('fsdp')
- grad_local_bias_mid: float32 [1024], P('fsdp')
- grad_local_w_in: float32 [1024, 4096], P('fsdp')
- grad_local_w_down: float32 [4096, 1024], P('fsdp')
- grad_recall_gain_in: float32 [1024], P('fsdp')
- grad_recall_bias_in: float32 [1024], P('fsdp')
- grad_recall_w_qkv: float32 [1024, 3072], P('fsdp')
- grad_recall_rel_bias: float32 [8, 32], P('fsdp')
- grad_recall_w_out: float32 [1024, 1024], P('fsdp')
- grad_recall_gain_mid: float32 [1024], P('fsdp')
- grad_recall_bias_mid: float32 [1024], P('fsdp')
- grad_recall_w_in: float32 [1024, 4096], P('fsdp')
- grad_recall_w_down: float32 [4096, 1024], P('fsdp')
- grad_recall_gate: float32 [8], P('fsdp')
The draws below stay inside these ranges and needn't reach their ends.
Inputs may be any that keep to these rules, and one draw needn't show every extreme that they name: `block_slots`: the two slots of every device of ctx (slots 2 c and 2 c + 1) hold stream blocks j and 15 - j; each block of a stream stands once. `doc_starts`: the first start is 0; the others do not fall and lie in the stream's second half; equal starts give empty documents.
All inputs are finite; a program needn't handle non-finite values.
Results may differ from the reference program's by a relative error of at most 0.034.
Values may be sent and summed in bfloat16 or wider, within the bound.
No kernel may reach another device: no remote copies, remote signals or barrier semaphores. Data moves between devices by JAX's collectives and lax.ppermute only.
A program may use at most 512 MiB of HBM per device.

```python
import math
import jax
import jax.numpy as jnp
import numpy as np
from jax import lax

D = 1024
HEADS = 8
HEAD_DIM = 128
FF = 4096
BUCKETS = 32
WIN = 512
BLK = 128
TOPK = 32
DOCS = 4
MICRO = 2
SEQS = 4
SLOTS = 16
STREAM = 2048
MEM = 2048


def draw_block_slots(key, part):
    key = jax.random.fold_in(key, 11)
    half_count = SLOTS // 2
    keys_all = jax.random.split(key, MICRO * SEQS)
    orders = jax.vmap(lambda sub_key: jax.random.permutation(sub_key, half_count))(keys_all).astype(jnp.int32)
    paired = jnp.stack([orders, SLOTS - 1 - orders], axis=-1)
    return paired.reshape(MICRO, SEQS, SLOTS).astype(jnp.int32)


def draw_doc_starts(key, part):
    key = jax.random.fold_in(key, 23)
    later = jax.random.randint(key, (MICRO, SEQS, DOCS - 1), STREAM // 2, STREAM).astype(jnp.int32)
    later = jnp.sort(later, axis=-1)
    return jnp.concatenate([jnp.zeros((MICRO, SEQS, 1), jnp.int32), later], -1)


def with_ends(values, rng, low, top_value):
    spot = [jax.random.randint(jax.random.fold_in(rng, axis), (), 0, length) for axis, length in enumerate(values.shape)]
    widest = values.shape.index(max(values.shape))
    neighbour = spot[:widest] + [(spot[widest] + 1) % values.shape[widest]] + spot[widest + 1:]
    return values.at[tuple(spot)].set(low).at[tuple(neighbour)].set(top_value)


def shard_levels(stream_key, shape, cuts, least, largest):
    def one(dim, shards_of):
        steps = jax.random.uniform(jax.random.fold_in(jax.random.fold_in(stream_key, 6), dim), (shards_of,), jnp.float32, least / len(cuts), largest / len(cuts))
        return jnp.repeat(jnp.exp(steps), shape[dim] // shards_of).reshape((-1,) + (1,) * (len(shape) - dim - 1))

    factor_of = one(*cuts[0])
    for cut in cuts[1:]:
        factor_of = factor_of * one(*cut)
    return factor_of


def bell_draw(rng, dims, deviation, limit, shards=(), kind=jnp.bfloat16):
    entries = jax.random.normal(rng, dims, jnp.float32) * deviation
    if len(shards) > 0:
        entries = shard_levels(rng, dims, shards, -0.22, 0.18) * entries
    return jnp.clip(entries, min=-limit, max=limit).astype(kind)


def setup_inputs(seed: int = 0) -> dict:
    key_of = jax.random.split(jax.random.key(seed), 27)
    inputs = bell_draw(key_of[0], (MICRO, SEQS, STREAM, D), 1.0, 6.0, ((1, 4), (2, 8)))
    block_slots = draw_block_slots(jax.random.fold_in(key_of[26], 71), 0)
    doc_starts = draw_doc_starts(jax.random.fold_in(key_of[26], 71), 0)
    mem_index = with_ends(jax.random.randint(key_of[3], (MICRO, SEQS, STREAM, HEADS, TOPK), 0, MEM), jax.random.fold_in(key_of[3], 1), 0, MEM - 1).astype(jnp.int32)
    mem_keys = bell_draw(key_of[4], (SEQS, MEM, D), 1.5, 8.0, ((0, 4), (1, 8)))
    mem_values = bell_draw(key_of[5], (SEQS, MEM, D), 1.0, 6.0, ((0, 4), (1, 8)))
    out_grad = bell_draw(key_of[6], (MICRO, SEQS, STREAM, D), 1.0, 6.0, ((1, 4), (2, 8)))
    local_gain_in = jnp.clip(1.0 + 0.1 * jax.random.normal(key_of[7], (D,), jnp.float32), 0.5, 1.5).astype(jnp.bfloat16)
    local_bias_in = bell_draw(key_of[8], (D,), 0.2, 1.25, ((0, 4),))
    local_w_qkv = bell_draw(key_of[9], (D, 3 * D), D ** -0.5, 0.1875, ((0, 4),))
    local_rel_bias = bell_draw(key_of[10], (HEADS, BUCKETS), 0.5, 3.0, ((0, 4),))
    local_w_out = bell_draw(key_of[11], (D, D), (D // 16) ** -0.5, 0.75, ((0, 4),))
    local_gain_mid = jnp.clip(1.0 + 0.1 * jax.random.normal(key_of[12], (D,), jnp.float32), 0.5, 1.5).astype(jnp.bfloat16)
    local_bias_mid = bell_draw(key_of[13], (D,), 0.2, 1.25, ((0, 4),))
    local_w_in = bell_draw(key_of[14], (D, FF), D ** -0.5, 0.1875, ((0, 4),))
    local_w_down = bell_draw(key_of[15], (FF, D), FF ** -0.5, 0.09375, ((0, 4),))
    recall_gain_in = jnp.clip(1.0 + 0.1 * jax.random.normal(key_of[16], (D,), jnp.float32), 0.5, 1.5).astype(jnp.bfloat16)
    recall_bias_in = bell_draw(key_of[17], (D,), 0.2, 1.25, ((0, 4),))
    recall_w_qkv = bell_draw(key_of[18], (D, 3 * D), D ** -0.5, 0.1875, ((0, 4),))
    recall_rel_bias = bell_draw(key_of[19], (HEADS, BUCKETS), 0.5, 3.0, ((0, 4),))
    recall_w_out = bell_draw(key_of[20], (D, D), (D // 16) ** -0.5, 0.75, ((0, 4),))
    recall_gain_mid = jnp.clip(1.0 + 0.1 * jax.random.normal(key_of[21], (D,), jnp.float32), 0.5, 1.5).astype(jnp.bfloat16)
    recall_bias_mid = bell_draw(key_of[22], (D,), 0.2, 1.25, ((0, 4),))
    recall_w_in = bell_draw(key_of[23], (D, FF), D ** -0.5, 0.1875, ((0, 4),))
    recall_w_down = bell_draw(key_of[24], (FF, D), FF ** -0.5, 0.09375, ((0, 4),))
    recall_gate = bell_draw(key_of[25], (HEADS,), 1.5, 8.0, ((0, 4),))
    return dict(inputs=inputs, block_slots=block_slots, doc_starts=doc_starts, mem_index=mem_index, mem_keys=mem_keys, mem_values=mem_values, out_grad=out_grad, local_gain_in=local_gain_in, local_bias_in=local_bias_in, local_w_qkv=local_w_qkv, local_rel_bias=local_rel_bias, local_w_out=local_w_out, local_gain_mid=local_gain_mid, local_bias_mid=local_bias_mid, local_w_in=local_w_in, local_w_down=local_w_down, recall_gain_in=recall_gain_in, recall_bias_in=recall_bias_in, recall_w_qkv=recall_w_qkv, recall_rel_bias=recall_rel_bias, recall_w_out=recall_w_out, recall_gain_mid=recall_gain_mid, recall_bias_mid=recall_bias_mid, recall_w_in=recall_w_in, recall_w_down=recall_w_down, recall_gate=recall_gate)


EPS = 1e-05
NEGATIVE = -1000000000.0
FAR_DISTANCE = 128
HIGH = lax.Precision.HIGHEST

@jax.custom_vjp
def low(v):
    return lax.optimization_barrier(v.astype(jnp.bfloat16)).astype(jnp.float32)

@jax.custom_vjp
def low_back(v):
    return v

def low_keep(v):
    return (low(v), None)

def low_pass(kept, grad):
    return (grad,)

def back_keep(v):
    return (v, None)

def back_low(kept, grad):
    return (low(grad),)
low.defvjp(low_keep, low_pass)
low_back.defvjp(back_keep, back_low)

def bucket_table(total_count, buckets):
    exact_count = buckets // 2
    result = []
    for distance in range(total_count):
        if distance < exact_count:
            result.append(distance)
        else:
            scaled = math.log(distance / exact_count) / math.log(FAR_DISTANCE / exact_count)
            result.append(min(exact_count + int(scaled * (buckets - exact_count)), buckets - 1))
    return np.array(result, dtype=np.int32)

def window_tables():
    reach_blocks = WIN // BLK
    span_keys = (reach_blocks + 1) * BLK
    distance = reach_blocks * BLK + np.arange(BLK)[:, None] - np.arange(span_keys)[None, :]
    inside = (distance >= 0) & (distance < WIN)
    buckets = bucket_table(WIN, BUCKETS)[np.clip(distance, 0, WIN - 1)]
    return (reach_blocks, span_keys, inside, buckets)

def norm_forward(vector, gain, offset):
    centre = vector - lax.optimization_barrier(jnp.mean(vector, -1, keepdims=True))
    spread = lax.optimization_barrier(jnp.mean(centre * centre, -1, keepdims=True))
    return centre * lax.rsqrt(spread + EPS) * gain + offset

def stack_window(padded, reach_blocks):
    return jnp.concatenate([padded[number:number + SLOTS] for number in range(reach_blocks + 1)], 1)

def recall_block(items, keys_mem, vals_mem):
    queries, rows_idx = items
    heads_idx = jnp.arange(HEADS)[None, :, None]
    mem_k = keys_mem.reshape(MEM, HEADS, HEAD_DIM)[rows_idx, heads_idx]
    mem_v = vals_mem.reshape(MEM, HEADS, HEAD_DIM)[rows_idx, heads_idx]
    mem_score = low_back(jnp.einsum('thd,thkd->thk', queries, mem_k, precision=HIGH) * HEAD_DIM ** (-0.5))
    mem_prob = jax.nn.softmax(mem_score, -1)
    return jnp.einsum('thk,thkd->thd', low(mem_prob), mem_v, precision=HIGH)

def one_layer(stream, doc_ids, params, memory_part):
    reach_blocks, span_keys, inside, buckets = window_tables()
    normed = low(norm_forward(stream, params[0], params[1]))
    qkv = low_back(low(jnp.dot(normed, params[2], precision=HIGH)))
    queries = qkv[:, :D].reshape(SLOTS, BLK, HEADS, HEAD_DIM)
    padded = jnp.concatenate([jnp.zeros((reach_blocks * BLK, 2 * D), jnp.float32), qkv[:, D:]], 0)
    window = stack_window(padded.reshape(SLOTS + reach_blocks, BLK, 2 * D), reach_blocks)
    key_win = window[..., :D].reshape(SLOTS, span_keys, HEADS, HEAD_DIM)
    val_win = window[..., D:].reshape(SLOTS, span_keys, HEADS, HEAD_DIM)
    doc_pad = jnp.concatenate([jnp.full((reach_blocks * BLK,), -1, jnp.int32), doc_ids.astype(jnp.int32)], 0)
    doc_win = stack_window(doc_pad.reshape(SLOTS + reach_blocks, BLK), reach_blocks)
    allowed = jnp.asarray(inside)[None] & (doc_ids.reshape(SLOTS, BLK)[:, :, None] == doc_win[:, None, :])
    rel_scores = jnp.take(params[3], jnp.asarray(buckets), axis=1)
    scores = jnp.einsum('bihd,bjhd->bhij', queries, key_win, precision=HIGH) * HEAD_DIM ** (-0.5) + rel_scores[None]
    scores = low_back(jnp.where(allowed[:, None], scores, NEGATIVE))
    attn_prob = jax.nn.softmax(scores, -1)
    local_out = jnp.einsum('bhij,bjhd->bihd', low(attn_prob), val_win, precision=HIGH)
    local_out = low_back(local_out.reshape(STREAM, HEADS, HEAD_DIM))
    if memory_part is None:
        mixed_heads = local_out
    else:
        keys_mem, vals_mem, rows_idx = memory_part
        recalled = lax.map(jax.checkpoint(partial_recall(keys_mem, vals_mem)), (queries, rows_idx.reshape(SLOTS, BLK, HEADS, TOPK)))
        mem_out = low_back(recalled.reshape(STREAM, HEADS, HEAD_DIM))
        gate_value = jax.nn.sigmoid(params[9])[None, :, None]
        mixed_heads = gate_value * mem_out + (1.0 - gate_value) * local_out
    mixed_low = low(mixed_heads.reshape(STREAM, D))
    hidden = stream + low_back(jnp.dot(mixed_low, params[4], precision=HIGH))
    normed_mid = low(norm_forward(hidden, params[5], params[6]))
    up_proj = low_back(jnp.dot(normed_mid, params[7], precision=HIGH))
    act_low = low(jax.nn.gelu(up_proj))
    return hidden + low_back(jnp.dot(act_low, params[8], precision=HIGH))

def partial_recall(keys_mem, vals_mem):

    def apply_block(items):
        return recall_block(items, keys_mem, vals_mem)
    return apply_block

def reorder(array_in, block_order):

    def single_item(item_array, item_order):
        blocks = item_array.reshape((item_order.shape[0], BLK) + item_array.shape[1:])
        return blocks[item_order].reshape(item_array.shape)
    return jax.vmap(jax.vmap(single_item))(array_in, block_order)

def reference(inputs, block_slots, doc_starts, mem_index, mem_keys, mem_values, out_grad, local_gain_in, local_bias_in, local_w_qkv, local_rel_bias, local_w_out, local_gain_mid, local_bias_mid, local_w_in, local_w_down, recall_gain_in, recall_bias_in, recall_w_qkv, recall_rel_bias, recall_w_out, recall_gain_mid, recall_bias_mid, recall_w_in, recall_w_down, recall_gate):
    raw_params = (local_gain_in, local_bias_in, local_w_qkv, local_rel_bias, local_w_out, local_gain_mid, local_bias_mid, local_w_in, local_w_down, recall_gain_in, recall_bias_in, recall_w_qkv, recall_rel_bias, recall_w_out, recall_gain_mid, recall_bias_mid, recall_w_in, recall_w_down, recall_gate)
    params = tuple((param.astype(jnp.float32) for param in raw_params))
    inverse = jnp.argsort(block_slots, axis=-1).astype(jnp.int32)
    stream_count = MICRO * SEQS
    rows_stream = reorder(mem_index, inverse).reshape(stream_count, STREAM, HEADS, TOPK)
    positions = jnp.arange(STREAM, dtype=jnp.int32)
    doc_ids = lax.optimization_barrier(jnp.sum((doc_starts[:, :, None, :] <= positions[None, None, :, None]).astype(jnp.int32), -1)) - 1
    doc_ids = doc_ids.reshape(stream_count, STREAM).astype(jnp.int32)
    keys_all = jnp.broadcast_to(mem_keys.astype(jnp.float32)[None], (MICRO, SEQS, MEM, D)).reshape(stream_count, MEM, D)
    vals_all = jnp.broadcast_to(mem_values.astype(jnp.float32)[None], (MICRO, SEQS, MEM, D)).reshape(stream_count, MEM, D)

    def forward_all(inputs_f32, weights_all):
        local_p = weights_all[:9]
        recall_p = weights_all[9:]
        streams = reorder(inputs_f32, inverse).reshape(stream_count, STREAM, D)

        def one_stream(items):
            stream, docs_one, rows_one, keys_one, vals_one = items
            first_out = one_layer(stream, docs_one, local_p, None)
            return one_layer(first_out, docs_one, recall_p, (keys_one, vals_one, rows_one))
        results = lax.map(jax.checkpoint(one_stream), (streams, doc_ids, rows_stream, keys_all, vals_all))
        return reorder(results.reshape(MICRO, SEQS, STREAM, D), block_slots)
    result_out, pull_back = jax.vjp(forward_all, inputs.astype(jnp.float32), params)
    input_grad, grads = pull_back(out_grad.astype(jnp.float32))
    return (result_out.astype(jnp.bfloat16), input_grad, grads[0], grads[1], grads[2], grads[3], grads[4], grads[5], grads[6], grads[7], grads[8], grads[9], grads[10], grads[11], grads[12], grads[13], grads[14], grads[15], grads[16], grads[17], grads[18])
```

```python
import functools
import math

import jax
import jax.numpy as jnp
import numpy as np
from jax import lax
from jax.experimental import pallas as pl
from jax.experimental.pallas import tpu as pltpu
from jax.sharding import PartitionSpec as P

HEADS = 8
HD = 128
BUCKETS = 32
WIN = 512
BLK = 128
TOPK = 32
SPAN = WIN + BLK
ROWS = 2 * BLK
LINE = 4
EPS = 1e-05
NEG = -1000000000.0
FAR_DISTANCE = 128
SCALE = HD ** (-0.5)
F32 = jnp.float32
BF16 = jnp.bfloat16
MIB = 1 << 20


def bucket_table(total_count, buckets):
    exact_count = buckets // 2
    result = []
    for distance in range(total_count):
        if distance < exact_count:
            result.append(distance)
        else:
            scaled = math.log(distance / exact_count) / math.log(FAR_DISTANCE / exact_count)
            result.append(min(exact_count + int(scaled * (buckets - exact_count)), buckets - 1))
    return np.array(result, dtype=np.int32)


def window_buckets():
    distance = WIN + np.arange(BLK)[:, None] - np.arange(SPAN)[None, :]
    inside = (distance >= 0) & (distance < WIN)
    buckets = bucket_table(WIN, BUCKETS)[np.clip(distance, 0, WIN - 1)]
    return np.where(inside, buckets, -1).astype(np.int32)


def dot(a, b):
    return lax.dot_general(a, b, (((1,), (0,)), ((), ())), preferred_element_type=F32)


def dot_nt(a, b):
    return lax.dot_general(a, b, (((1,), (1,)), ((), ())), preferred_element_type=F32)


def dot_tn(a, b):
    return lax.dot_general(a, b, (((0,), (0,)), ((), ())), preferred_element_type=F32)


def params(mib):
    return pltpu.CompilerParams(vmem_limit_bytes=mib * MIB)


def cost(flops, nbytes):
    return pl.CostEstimate(flops=int(flops), bytes_accessed=int(nbytes), transcendentals=0)


def vmem():
    return pl.BlockSpec(memory_space=pltpu.VMEM)


def smem():
    return pl.BlockSpec(memory_space=pltpu.SMEM)


def anyspace():
    return pl.BlockSpec(memory_space=pl.ANY)


def shape(dims, kind):
    return jax.ShapeDtypeStruct(tuple(dims), kind)


def whole(dims):
    zeros = (0,) * len(dims)
    return pl.BlockSpec(tuple(dims), lambda *_: zeros)


def single(dims):
    zeros = (0,) * len(dims)
    return pl.BlockSpec(tuple(dims), lambda _: zeros)


def xor_perm(count, bit):
    return [(i, i ^ bit) for i in range(count)]


def bit_list(count):
    bits = []
    bit = 1
    while bit < count:
        bits.append(bit)
        bit *= 2
    return bits


def swap_ctx(x, bit):
    return lax.ppermute(x, "ctx", xor_perm(lax.axis_size("ctx"), bit))


def swap_fsdp(x, bit):
    return lax.ppermute(x, "fsdp", xor_perm(lax.axis_size("fsdp"), bit))


def exchange(x):
    return lax.all_to_all(x, "ctx", 0, 0, tiled=False)


def side_columns(side, half):
    return pl.ds(pl.multiple_of(side * half, HD), half)


def pack_kernel(plan, key, *refs):
    weights, out, held, sems = refs[:-3], refs[-3], refs[-2], refs[-1]
    copies = []
    for n, (i, row, rows, half, to_row, to_column) in enumerate(plan):
        copies.append(
            pltpu.make_async_copy(
                weights[i].at[row : row + rows, side_columns(key[0], half)],
                held.at[to_row : to_row + rows, to_column : to_column + half],
                sems.at[n],
            )
        )
    for copy in copies:
        copy.start()
    for copy in copies:
        copy.wait()
    last = pltpu.make_async_copy(held, out, sems.at[len(plan)])
    last.start()
    last.wait()


def pack(weights, plan, rows, core):
    columns = max(to_column + half for *_, half, _, to_column in plan)
    dims = (rows, columns)
    return pl.pallas_call(
        functools.partial(pack_kernel, plan),
        in_specs=[smem()] + [anyspace()] * len(weights),
        out_specs=anyspace(),
        out_shape=shape(dims, BF16),
        scratch_shapes=[pltpu.VMEM(dims, BF16), pltpu.SemaphoreType.DMA((len(plan) + 1,))],
        compiler_params=params(56),
        cost_estimate=cost(0, 4 * rows * columns),
        name="pack",
    )(core, *weights)


def unfold_kernel(count, plan, shards, key, mine, twin, *refs):
    total = len(shards)
    outs, held, arrive, leave = refs[:total], refs[total : 2 * total], refs[-2], refs[-1]
    groups, n = [], 0
    for i, shard in enumerate(shards):
        for f in range(count):
            copies = []
            for j, row, rows, half, from_row, from_column in plan:
                if j != i:
                    continue
                for ref, side in ((mine, key[0]), (twin, 1 - key[0])):
                    copies.append(
                        pltpu.make_async_copy(
                            ref.at[f, from_row : from_row + rows, from_column : from_column + half],
                            held[i].at[
                                f * shard + row : f * shard + row + rows, side_columns(side, half)
                            ],
                            arrive.at[n],
                        )
                    )
                    n += 1
            span = slice(f * shard, (f + 1) * shard)
            groups.append(
                (copies, pltpu.make_async_copy(held[i].at[span], outs[i].at[span], leave.at[len(groups)]))
            )
    for copies, _ in groups:
        for copy in copies:
            copy.start()
    for copies, last in groups:
        for copy in copies:
            copy.wait()
        last.start()
    for _, last in groups:
        last.wait()


def unfold_weights(mine, weights, plan, core):
    count = lax.axis_size("fsdp")
    twin = swap_ctx(mine, 1)
    shards = [w.shape[0] for w in weights]
    full = [(w.shape[0] * count, w.shape[1]) for w in weights]
    return pl.pallas_call(
        functools.partial(unfold_kernel, count, plan, shards),
        out_shape=[shape(dims, BF16) for dims in full],
        in_specs=[smem(), anyspace(), anyspace()],
        out_specs=[anyspace()] * len(full),
        scratch_shapes=[pltpu.VMEM(dims, BF16) for dims in full]
        + [
            pltpu.SemaphoreType.DMA((2 * count * len(plan),)),
            pltpu.SemaphoreType.DMA((count * len(full),)),
        ],
        compiler_params=params(60),
        cost_estimate=cost(0, 8 * mine.size),
        name="unfold",
    )(core, mine, twin)


def merge(mine, twin, plan, dims, core):
    half = len(mine)

    def body(key, *refs):
        first, second, outs = refs[:half], refs[half : 2 * half], refs[2 * half :]
        for source, side in ((first, key[0]), (second, 1 - key[0])):
            for i, row, rows, width, n, from_row, from_column, offset, size in plan:
                column = pl.multiple_of(side * width + offset, HD)
                outs[i][row : row + rows, pl.ds(column, size)] = source[n][
                    from_row : from_row + rows, from_column : from_column + size
                ].astype(F32)

    return pl.pallas_call(
        body,
        grid=(1,),
        in_specs=[smem()] + [single(x.shape) for x in (*mine, *twin)],
        out_specs=[single(d) for d in dims],
        out_shape=[shape(d, F32) for d in dims],
        compiler_params=params(56),
        cost_estimate=cost(0, sum(8 * a * b for a, b in dims)),
        name="merge",
    )(core, *mine, *twin)


def fetch_small(vector):
    count = lax.axis_size("fsdp")
    have = {0: vector}
    for bit in bit_list(count):
        for r in list(have):
            have[r ^ bit] = swap_fsdp(have[r], bit)
    stacked = jnp.stack([have[r] for r in range(count)])
    return jnp.take(stacked, lax.axis_index("fsdp") ^ jnp.arange(count), axis=0)


def add_terms(terms):
    total = terms[0].astype(F32)
    for term in terms[1:]:
        total = total + term.astype(F32)
    return total.astype(BF16)


def reduce_steps(keep, send, bits):
    count = lax.axis_size("fsdp")
    ctx_count = lax.axis_size("ctx")
    me_ctx = lax.axis_index("ctx")
    core = me_ctx & 1
    z = (me_ctx >> 1) & (LINE - 1)
    terms = [keep, (yield "ctx", xor_perm(ctx_count, 1), send)]
    left = count
    for bit in bits:
        left //= 2
        got = yield "fsdp", xor_perm(count, bit), add_terms([t[left:] for t in terms])
        terms = [t[:left] for t in terms] + [got]
    mine = add_terms([t[0] for t in terms])

    def along(pairs):
        stride = 2 * LINE
        return [
            (g * stride + 2 * a + c, g * stride + 2 * b + c)
            for g in range(ctx_count // stride)
            for a, b in pairs
            for c in range(2)
        ]

    inner = add_terms([mine, (yield "ctx", along([(0, 1), (3, 2)]), mine)])
    both = add_terms([inner, (yield "ctx", along([(1, 2), (2, 1)]), inner)])
    outer = yield "ctx", along([(1, 0), (2, 3)]), both
    full = jnp.where((z == 0) | (z == LINE - 1), outer, both)
    bit = 2 * LINE
    while bit < ctx_count:
        full = add_terms([full, (yield "ctx", xor_perm(ctx_count, bit), full)])
        bit *= 2
    return full, (yield "ctx", xor_perm(ctx_count, 1), full)


def sum_lines(mine):
    ctx_count = lax.axis_size("ctx")
    groups = [[g for g in range(ctx_count) if g % 2 == c] for c in range(2)]
    return lax.psum(mine, "ctx", axis_index_groups=groups)


class Lane:
    def __init__(self):
        self.active = []
        self.done = {}

    def add(self, key, steps):
        self.active.append((key, steps, next(steps)))

    def drain(self):
        while self.active:
            left = []
            for key, steps, (axis, pairs, operand) in self.active:
                try:
                    left.append((key, steps, steps.send(lax.ppermute(operand, axis, pairs))))
                except StopIteration as stop:
                    self.done[key] = stop.value
            self.active = left


def grad_kernel(key, a0, a1, k0, k1, s0, s1, *refs):
    keep, send = refs[-2:]
    left0, left1 = a0[...], a1[...]
    keep[0] = (dot_tn(left0, k0[...]) + dot_tn(left1, k1[...])).astype(BF16)
    send[0] = (dot_tn(left0, s0[...]) + dot_tn(left1, s1[...])).astype(BF16)


def shard_order(bits):
    order = [0]
    for bit in reversed(bits):
        order = order + [r | bit for r in order]
    return order


def weight_grad(a, b, shard, tile, first, tiles, bits=None, into=None, place=(0, 0), dims=None):
    count = lax.axis_size("fsdp")
    me = lax.axis_index("fsdp")
    core = lax.axis_index("ctx") & 1
    rows, width = b[0].shape
    across = width // 2 // tile
    chunks = a[0].shape[1] // (count * shard)
    order = jnp.arange(count) if bits is None else me ^ jnp.array(shard_order(bits))
    key = jnp.concatenate([core.reshape(1), order]).astype(jnp.int32)
    dims = dims or (count, shard, chunks * tiles * tile)
    row, column = place
    a_spec = pl.BlockSpec((rows, shard), lambda i, t, k: (0, k[1 + i] * chunks + t // tiles))

    def b_spec(twin):
        return pl.BlockSpec(
            (rows, tile),
            lambda i, t, k: (0, (1 - k[0] if twin else k[0]) * across + first + t % tiles),
        )

    o_spec = pl.BlockSpec((1, shard, tile), lambda i, t, k: (i, row, column + t))
    extra = list(into or [])
    return pl.pallas_call(
        grad_kernel,
        grid_spec=pltpu.PrefetchScalarGridSpec(
            num_scalar_prefetch=1,
            grid=(count, chunks * tiles),
            in_specs=[a_spec, a_spec, b_spec(False), b_spec(False), b_spec(True), b_spec(True)]
            + [anyspace()] * len(extra),
            out_specs=[o_spec, o_spec],
        ),
        out_shape=[shape(dims, BF16)] * 2,
        input_output_aliases={7: 0, 8: 1} if extra else {},
        compiler_params=params(56),
        cost_estimate=cost(
            8 * rows * shard * count * chunks * tiles * tile,
            4 * shard * count * chunks * tiles * tile + 8 * rows * width,
        ),
        name="weight_grad",
    )(key, a[0], a[1], b[0], b[1], b[0], b[1], *extra)


def norm_parts(x):
    centre = x - jnp.mean(x, -1, keepdims=True)
    rstd = lax.rsqrt(jnp.mean(centre * centre, -1, keepdims=True) + EPS)
    return centre * rstd, rstd


def norm_back(x, gain, grad):
    hat, rstd = norm_parts(x)
    scaled = grad * gain
    out = rstd * (
        scaled
        - jnp.mean(scaled, -1, keepdims=True)
        - hat * jnp.mean(scaled * hat, -1, keepdims=True)
    )
    grad_gain = jnp.sum(grad * hat, 0, keepdims=True)
    grad_bias = jnp.sum(grad, 0, keepdims=True)
    return out, grad_gain, grad_bias


GROUP = 4


def qkv_kernel(x_ref, gain, bias, weight, normed, pieces):
    @pl.when(pl.program_id(0) == 0)
    def _():
        hat, _ = norm_parts(x_ref[...].astype(F32))
        normed[...] = (hat * gain[...] + bias[...]).astype(BF16)

    group = dot(normed[...], weight[...]).astype(BF16)
    for copy in range(pieces.shape[0]):
        for h in range(GROUP):
            pieces[copy, h] = group[:, h * HD : (h + 1) * HD]


def qkv_forward(x, gain, bias, weight):
    count = lax.axis_size("ctx")
    width = x.shape[1]
    parts = HEADS // GROUP
    copies = count // HEADS
    normed, pieces = pl.pallas_call(
        qkv_kernel,
        grid=(3 * parts,),
        in_specs=[
            whole(x.shape),
            whole((1, width)),
            whole((1, width)),
            pl.BlockSpec((width, GROUP * HD), lambda t: (0, t)),
        ],
        out_specs=[
            whole((ROWS, width)),
            pl.BlockSpec((copies, GROUP, ROWS, HD), lambda t: (0, t % parts, 0, t // parts)),
        ],
        out_shape=[shape((ROWS, width), BF16), shape((copies, HEADS, ROWS, 3 * HD), BF16)],
        compiler_params=params(56),
        cost_estimate=cost(6 * ROWS * width * width, 8 * width * width),
        name="qkv",
    )(x, gain, bias, weight)
    return normed, pieces.reshape(count, ROWS, 3 * HD)


def gelu(u):
    inner = math.sqrt(2.0 / math.pi) * (u + 0.044715 * u * u * u)
    return 0.5 * u * (1.0 + jnp.tanh(inner))


def gelu_slope(u):
    c = math.sqrt(2.0 / math.pi)
    square = u * u
    t = jnp.tanh(c * (u + 0.044715 * u * square))
    return 0.5 * (1.0 + t) + 0.5 * u * (1.0 - t * t) * (c * (1.0 + 3.0 * 0.044715 * square))


def mlp_kernel(steps, x_ref, w_out, gain, bias, w_in, w_down, pieces, *refs):
    mixed, hidden, normed, up, act, out, total = refs
    step = pl.program_id(0)

    @pl.when(step == 0)
    def _():
        for s in range(HEADS):
            mixed[:, s * HD : (s + 1) * HD] = pieces[s]
        h = x_ref[...].astype(F32) + dot(mixed[...], w_out[...])
        hidden[...] = h
        hat, _ = norm_parts(h)
        normed[...] = (hat * gain[...] + bias[...]).astype(BF16)
        total[...] = h

    u = dot(normed[...], w_in[...])
    up[...] = u.astype(BF16)
    a = gelu(u).astype(BF16)
    act[...] = a
    total[...] += dot(a, w_down[...])

    @pl.when(step == steps - 1)
    def _():
        out[...] = total[...].astype(out.dtype)


def mlp_forward(x, pieces, w_out, gain, bias, w_in, w_down, kind):
    width = x.shape[1]
    ff = w_in.shape[1]
    tile = 512
    steps = ff // tile
    row = (ROWS, width)
    return pl.pallas_call(
        functools.partial(mlp_kernel, steps),
        grid=(steps,),
        in_specs=[
            whole(row),
            whole(w_out.shape),
            whole((1, width)),
            whole((1, width)),
            pl.BlockSpec((width, tile), lambda j: (0, j)),
            pl.BlockSpec((tile, width), lambda j: (j, 0)),
            whole((HEADS, ROWS, HD)),
        ],
        out_specs=[
            whole(row),
            whole(row),
            whole(row),
            pl.BlockSpec((ROWS, tile), lambda j: (0, j)),
            pl.BlockSpec((ROWS, tile), lambda j: (0, j)),
            whole(row),
        ],
        scratch_shapes=[pltpu.VMEM(row, F32)],
        out_shape=[
            shape(row, BF16),
            shape(row, F32),
            shape(row, BF16),
            shape((ROWS, ff), BF16),
            shape((ROWS, ff), BF16),
            shape(row, kind),
        ],
        compiler_params=params(56),
        cost_estimate=cost(2 * ROWS * width * (width + 2 * ff), 2 * width * (width + 2 * ff)),
        name="mlp",
    )(x, w_out, gain, bias, w_in, w_down, pieces)


def mlp_back_kernel(steps, g_ref, up, w_in, w_down, hidden, gain, w_out, *refs):
    du, grad_low, grad_hidden, grad_gain, grad_bias, pieces, total, low = refs
    step = pl.program_id(0)

    @pl.when(step == 0)
    def _():
        low[...] = g_ref[...].astype(BF16)
        total[...] = jnp.zeros_like(total)

    d_act = dot_nt(low[...], w_down[...])
    d_up = (gelu_slope(up[...].astype(F32)) * d_act).astype(BF16)
    du[...] = d_up
    total[...] += dot_nt(d_up, w_in[...])

    @pl.when(step == steps - 1)
    def _():
        part, g_gain, g_bias = norm_back(hidden[...], gain[...], total[...])
        grad_gain[...] = g_gain
        grad_bias[...] = g_bias
        dh = g_ref[...].astype(F32) + part
        grad_hidden[...] = dh
        hb = dh.astype(BF16)
        grad_low[...] = hb
        mixed = dot_nt(hb, w_out[...]).astype(BF16)
        for s in range(pieces.shape[0]):
            h = s % HEADS
            pieces[s] = mixed[:, h * HD : (h + 1) * HD]


def mlp_backward(grad, up, w_in, w_down, hidden, gain, w_out):
    count = lax.axis_size("ctx")
    width = hidden.shape[1]
    ff = w_in.shape[1]
    tile = 512
    steps = ff // tile
    row = (ROWS, width)
    return pl.pallas_call(
        functools.partial(mlp_back_kernel, steps),
        grid=(steps,),
        in_specs=[
            whole(row),
            pl.BlockSpec((ROWS, tile), lambda j: (0, j)),
            pl.BlockSpec((width, tile), lambda j: (0, j)),
            pl.BlockSpec((tile, width), lambda j: (j, 0)),
            whole(row),
            whole((1, width)),
            whole(w_out.shape),
        ],
        out_specs=[
            pl.BlockSpec((ROWS, tile), lambda j: (0, j)),
            whole(row),
            whole(row),
            whole((1, width)),
            whole((1, width)),
            whole((count, ROWS, HD)),
        ],
        scratch_shapes=[pltpu.VMEM(row, F32), pltpu.VMEM(row, BF16)],
        out_shape=[
            shape((ROWS, ff), BF16),
            shape(row, BF16),
            shape(row, F32),
            shape((1, width), F32),
            shape((1, width), F32),
            shape((count, ROWS, HD), BF16),
        ],
        compiler_params=params(56),
        cost_estimate=cost(2 * ROWS * width * (width + 2 * ff), 2 * width * (width + 2 * ff)),
        name="mlp_back",
    )(grad, up, w_in, w_down, hidden, gain, w_out)


def qkv_back_kernel(x_ref, gain, grad_hidden, weight, pieces, *refs):
    dqkv, grad_x, grad_low, grad_gain, grad_bias, total = refs
    step = pl.program_id(0)

    @pl.when(step == 0)
    def _():
        total[...] = jnp.zeros_like(total)

    for h in range(GROUP):
        dqkv[:, h * HD : (h + 1) * HD] = pieces[h]
    total[...] += dot_nt(dqkv[...], weight[...])

    @pl.when(step == pl.num_programs(0) - 1)
    def _():
        part, g_gain, g_bias = norm_back(x_ref[...].astype(F32), gain[...], total[...])
        grad_gain[...] = g_gain
        grad_bias[...] = g_bias
        result = grad_hidden[...] + part
        grad_x[...] = result
        grad_low[...] = result.astype(BF16)


def qkv_backward(x, gain, grad_hidden, weight, pieces):
    width = x.shape[1]
    row = (ROWS, width)
    parts = HEADS // GROUP
    wide = GROUP * HD
    return pl.pallas_call(
        qkv_back_kernel,
        grid=(3 * parts,),
        in_specs=[
            whole(row),
            whole((1, width)),
            whole(row),
            pl.BlockSpec((width, wide), lambda t: (0, t)),
            pl.BlockSpec((GROUP, ROWS, HD), lambda t: (t % parts, 0, t // parts)),
        ],
        out_specs=[
            pl.BlockSpec((ROWS, wide), lambda t: (0, t)),
            whole(row),
            whole(row),
            whole((1, width)),
            whole((1, width)),
        ],
        scratch_shapes=[pltpu.VMEM(row, F32)],
        out_shape=[
            shape((ROWS, 3 * width), BF16),
            shape(row, F32),
            shape(row, BF16),
            shape((1, width), F32),
            shape((1, width), F32),
        ],
        compiler_params=params(56),
        cost_estimate=cost(6 * ROWS * width * width, 6 * width * width),
        name="qkv_back",
    )(x, gain, grad_hidden, weight, pieces)


CHUNK = 64


def pick_scores(score_ref, index_ref, base, chunk):
    rows = pl.ds(pl.multiple_of(chunk * CHUNK, CHUNK), CHUNK)
    index = index_ref[pl.ds(pl.multiple_of(base + chunk * CHUNK, CHUNK), CHUNK), :]
    low = index & (HD - 1)
    high = index >> 7
    found = jnp.zeros((CHUNK, HD), F32)
    for tile in range(score_ref.shape[1] // HD):
        part = jnp.take_along_axis(
            score_ref[rows, tile * HD : (tile + 1) * HD], low, axis=1, mode="promise_in_bounds"
        )
        found = jnp.where(high == tile, part, found)
    return found


def scatter_rows(value_ref, value_base, index_ref, flat_ref, base, dense_ref, group):
    wide = 2 * HD
    start = pl.multiple_of(base + group * 16, 16)
    values = value_ref[pl.ds(pl.multiple_of(value_base + group * 16, 16), 16), :].astype(BF16)
    high = (index_ref[pl.ds(start, 16), :] >> 8).astype(F32).astype(BF16)
    query = lax.broadcasted_iota(jnp.int32, (16, HD), 0)
    lane = lax.broadcasted_iota(jnp.int32, (16, HD), 1) >> 5
    zero = jnp.zeros((16, HD), BF16)
    spots = [
        values * (query == lane + 4 * u).astype(F32).astype(BF16) for u in range(4)
    ]
    bands = []
    for h in range(dense_ref.shape[1] // wide):
        hit = high == jnp.array(h, BF16)
        bands.append(jnp.concatenate([jnp.where(hit, spot, zero) for spot in spots], 1))
    left = jnp.concatenate(bands, 0)
    flat = (flat_ref[pl.ds(pl.multiple_of((base + group * 16) // 4, 4), 4), :] & (wide - 1)).astype(F32).astype(BF16)
    place = lax.broadcasted_iota(jnp.int32, (wide, HD), 0).astype(F32).astype(BF16)
    one, none = jnp.ones((wide, HD), BF16), jnp.zeros((wide, HD), BF16)
    right = jnp.concatenate(
        [jnp.where(place == flat[u : u + 1, :], one, none) for u in range(4)], 1
    )
    spreadout = dot_nt(left, right)
    rows = pl.ds(pl.multiple_of(group * 16, 16), 16)
    for h in range(dense_ref.shape[1] // wide):
        dense_ref[rows, h * wide : (h + 1) * wide] = spreadout[h * 16 : (h + 1) * 16, :].astype(BF16)


def attend_kernel(recall, count, info, rel, buckets, pieces, *refs):
    if recall:
        mem, index, flat = refs[:3]
        refs = refs[3:]
    queries, keys, values, probs, outs = refs[:5]
    refs = refs[5:]
    if recall:
        weights, gap, mixed, bias, scores, dense = refs
    else:
        mixed, bias = refs

    def table(n, carry):
        rows = pl.ds(pl.multiple_of(n * 8, 8), 8)
        bucket = buckets[rows, :]
        part = jnp.full(bucket.shape, NEG, F32)
        for b in range(BUCKETS):
            part = jnp.where(bucket == b, rel[b], part)
        bias[rows, :] = part
        return carry

    lax.fori_loop(0, BLK // 8, table, 0)
    keys[0:WIN, :] = jnp.zeros((WIN, HD), BF16)
    values[0:WIN, :] = jnp.zeros((WIN, HD), BF16)
    for s in range(count):
        queries[s * ROWS : (s + 1) * ROWS, :] = pieces[s, :, :HD]
        for half in range(2):
            row = pl.multiple_of(info[2 * s + half] * BLK + WIN, BLK)
            span = slice(half * BLK, (half + 1) * BLK)
            keys[pl.ds(row, BLK), :] = pieces[s, span, HD : 2 * HD]
            values[pl.ds(row, BLK), :] = pieces[s, span, 2 * HD :]

    def one(s, carry):
        base = pl.multiple_of(s * ROWS, ROWS)
        for half in range(2):
            block = info[2 * s + half]
            row = pl.multiple_of(block * BLK, BLK)
            mine = pl.ds(pl.multiple_of(base + half * BLK, BLK), BLK)
            score = dot_nt(queries[mine, :], keys[pl.ds(row, SPAN), :]) * SCALE + bias[...]
            at = row + lax.broadcasted_iota(jnp.int32, (BLK, 1), 0)
            begin = jnp.zeros((BLK, 1), jnp.int32)
            for d in range(4):
                start = info[2 * count + d]
                begin = jnp.where(at >= start, jnp.maximum(begin, start), begin)
            key_at = row - WIN + lax.broadcasted_iota(jnp.int32, (1, SPAN), 1)
            score = jnp.where(key_at >= begin, score, NEG)
            exps = jnp.exp(score - jnp.max(score, -1, keepdims=True))
            prob = (exps * (1.0 / jnp.sum(exps, -1, keepdims=True))).astype(BF16)
            probs[2 * s + half] = prob
            mixed[mine, :] = dot(prob, values[pl.ds(row, SPAN), :])
        if recall:
            tile = pl.ds(base, ROWS)
            scores[...] = dot_nt(queries[tile, :], mem[:, :HD]) * SCALE

            def choose(chunk, inner):
                found = pick_scores(scores, index, base, chunk)
                exps = jnp.exp(found - jnp.max(found, -1, keepdims=True))
                weight = exps * ((HD // TOPK) / jnp.sum(exps, -1, keepdims=True))
                weights[pl.ds(pl.multiple_of(base + chunk * CHUNK, CHUNK), CHUNK), :] = weight
                return inner

            lax.fori_loop(0, ROWS // CHUNK, choose, 0)

            def place(group, inner):
                scatter_rows(weights, base, index, flat, base, dense, group)
                return inner

            lax.fori_loop(0, ROWS // 16, place, 0)
            found = dot(dense[...], mem[:, HD:])
            near = mixed[tile, :]
            gap[tile, :] = found - near
            gate = rel[BUCKETS]
            mixed[tile, :] = gate * found + (1.0 - gate) * near
        return carry

    lax.fori_loop(0, count, one, 0)
    for s in range(count):
        outs[s] = mixed[s * ROWS : (s + 1) * ROWS, :].astype(BF16)


def attend(pieces, info, rel, buckets, memory):
    count = lax.axis_size("ctx")
    total = count * ROWS
    recall = memory is not None
    operands = [info, rel, buckets, pieces]
    outs = [
        shape((total, HD), BF16),
        shape((total + WIN, HD), BF16),
        shape((total + WIN, HD), BF16),
        shape((2 * count, BLK, SPAN), BF16),
        shape((count, ROWS, HD), BF16),
    ]
    scratch = [pltpu.VMEM((total, HD), F32), pltpu.VMEM((BLK, SPAN), F32)]
    if recall:
        operands += list(memory)
        outs += [shape((total, HD), F32), shape((total, HD), F32)]
        rows = memory[0].shape[0]
        scratch += [pltpu.VMEM((ROWS, rows), F32), pltpu.VMEM((ROWS, rows), BF16)]
    result = pl.pallas_call(
        functools.partial(attend_kernel, recall, count),
        grid=(1,),
        in_specs=[smem(), smem()] + [single(x.shape) for x in operands[2:]],
        out_specs=[single(x.shape) for x in outs],
        out_shape=outs,
        scratch_shapes=scratch,
        compiler_params=params(60),
        cost_estimate=cost(45e9 if recall else 12e9, 8e6),
        name="recall_attend" if recall else "local_attend",
    )(*operands)
    return list(result[:4]) + list(result[5:]), result[4]


def attend_back_kernel(recall, count, info, rel, buckets, pieces, *refs):
    queries, keys, values, probs = refs[:4]
    refs = refs[4:]
    if recall:
        weights, gap, mem, index, flat, grad_rel, gate_sum = refs[:7]
        refs = refs[7:]
    else:
        grad_rel, refs = refs[0], refs[1:]
    outs, spread_sum, grads, dq, dk, dv = refs[:6]
    if recall:
        scores, dense, picked, mem_low = refs[6:]
        gate_sum[...] = jnp.zeros_like(gate_sum)
        gate = rel[BUCKETS]

    for s in range(count):
        grads[s * ROWS : (s + 1) * ROWS, :] = pieces[s]
    dk[...] = jnp.zeros_like(dk)
    dv[...] = jnp.zeros_like(dv)
    spread_sum[...] = jnp.zeros_like(spread_sum)

    def one(s, carry):
        base = pl.multiple_of(s * ROWS, ROWS)
        for half in range(2):
            block = info[2 * s + half]
            row = pl.multiple_of(block * BLK, BLK)
            mine = pl.ds(pl.multiple_of(base + half * BLK, BLK), BLK)
            near = pl.ds(row, SPAN)
            grad = grads[mine, :]
            if recall:
                grad = ((1.0 - gate) * grad.astype(F32)).astype(BF16)
            prob_low = probs[2 * s + half]
            prob = prob_low.astype(F32)
            d_prob = dot_nt(grad, values[near, :])
            product = prob * d_prob
            d_score = product - prob * jnp.sum(product, -1, keepdims=True)
            spread_sum[...] += d_score
            low = d_score.astype(BF16)
            dq[mine, :] = dot(low, keys[near, :]) * SCALE
            dk[near, :] += dot_tn(low, queries[mine, :]) * SCALE
            dv[near, :] += dot_tn(prob_low, grad)
        if recall:
            tile = pl.ds(base, ROWS)
            grad = grads[tile, :].astype(F32)
            gate_sum[...] += jnp.sum((grad * gap[tile, :]).reshape(ROWS // 8, 8, HD), 0)
            mem_low[...] = (gate * grad).astype(BF16)
            scores[...] = dot_nt(mem_low[...], mem[:, HD:])

            def choose(chunk, inner):
                found = pick_scores(scores, index, base, chunk)
                rows = pl.ds(pl.multiple_of(base + chunk * CHUNK, CHUNK), CHUNK)
                weight = weights[rows, :]
                product = weight * found
                centre = jnp.sum(product, -1, keepdims=True) * (TOPK / HD)
                local_rows = pl.ds(pl.multiple_of(chunk * CHUNK, CHUNK), CHUNK)
                picked[local_rows, :] = product - weight * centre
                return inner

            lax.fori_loop(0, ROWS // CHUNK, choose, 0)

            def place(group, inner):
                scatter_rows(picked, 0, index, flat, base, dense, group)
                return inner

            lax.fori_loop(0, ROWS // 16, place, 0)
            dq[tile, :] += dot(dense[...], mem[:, :HD]) * SCALE
        return carry

    lax.fori_loop(0, count, one, 0)
    for b in range(BUCKETS):
        part = jnp.sum(jnp.where(buckets[...] == b, spread_sum[...], 0.0), 0, keepdims=True)
        line = part[:, :HD]
        for n in range(1, SPAN // HD):
            line = line + part[:, n * HD : (n + 1) * HD]
        grad_rel[b : b + 1, :] = line
    for s in range(count):
        outs[s, :, :HD] = dq[s * ROWS : (s + 1) * ROWS, :].astype(BF16)
        for half in range(2):
            row = pl.multiple_of(info[2 * s + half] * BLK + WIN, BLK)
            span = slice(half * BLK, (half + 1) * BLK)
            outs[s, span, HD : 2 * HD] = dk[pl.ds(row, BLK), :].astype(BF16)
            outs[s, span, 2 * HD :] = dv[pl.ds(row, BLK), :].astype(BF16)


def attend_back(pieces, info, rel, buckets, saved, memory):
    count = lax.axis_size("ctx")
    total = count * ROWS
    recall = memory is not None
    operands = [info, rel, buckets, pieces, *saved]
    outs = [shape((BUCKETS, HD), F32)]
    scratch = [
        pltpu.VMEM((BLK, SPAN), F32),
        pltpu.VMEM((total, HD), BF16),
        pltpu.VMEM((total, HD), F32),
        pltpu.VMEM((total + WIN, HD), F32),
        pltpu.VMEM((total + WIN, HD), F32),
    ]
    if recall:
        operands += list(memory)
        rows = memory[0].shape[0]
        outs += [shape((8, HD), F32)]
        scratch += [
            pltpu.VMEM((ROWS, rows), F32),
            pltpu.VMEM((ROWS, rows), BF16),
            pltpu.VMEM((ROWS, HD), F32),
            pltpu.VMEM((ROWS, HD), BF16),
        ]
    outs += [shape((count, ROWS, 3 * HD), BF16)]
    result = pl.pallas_call(
        functools.partial(attend_back_kernel, recall, count),
        grid=(1,),
        in_specs=[smem(), smem()] + [single(x.shape) for x in operands[2:]],
        out_specs=[single(x.shape) for x in outs],
        out_shape=outs,
        scratch_shapes=scratch,
        compiler_params=params(60),
        cost_estimate=cost(50e9 if recall else 20e9, 8e6),
        name="recall_back" if recall else "local_back",
    )(*operands)
    return list(result[:-1]), result[-1]


def memory_rows(keys, values):
    count = lax.axis_size("ctx")

    def pieces(array):
        return [array[:, h * HD : (h + 1) * HD] for h in range(HEADS)]

    both = [jnp.concatenate(pair, 1) for pair in zip(pieces(keys), pieces(values))]
    stacked = jnp.stack(both * (count // HEADS))
    return exchange(stacked).reshape(count * ROWS, 2 * HD)


def memory_index(mem_index):
    count = lax.axis_size("ctx")
    micro = mem_index.shape[0]
    by_head = jnp.transpose(mem_index, (2, 0, 1, 3)).reshape(HEADS, micro, ROWS * TOPK // HD, HD)
    got = exchange(jnp.concatenate([by_head] * (count // HEADS), 0))
    result = []
    for m in range(micro):
        flat = got[:, m].reshape(-1, HD)
        index = jnp.tile(flat.reshape(count * ROWS, TOPK), (1, HD // TOPK))
        result.append((index, flat))
    return result


def local(
    inputs,
    block_slots,
    doc_starts,
    mem_index,
    mem_keys,
    mem_values,
    out_grad,
    *weights,
):
    me = lax.axis_index("ctx")
    me_fsdp = lax.axis_index("fsdp")
    count = lax.axis_size("ctx")
    fsdp = lax.axis_size("fsdp")
    micro = inputs.shape[0]
    width = inputs.shape[-1]
    my_head = me & (HEADS - 1)

    layers = [list(weights[:9]), list(weights[9:19])]
    small_of = [[0, 1, 5, 6, 3], [0, 1, 5, 6, 3, 9]]
    small = jnp.concatenate(
        [layers[n][i].reshape(-1) for n in range(2) for i in small_of[n]]
    )
    lengths = [layers[n][i].size for n in range(2) for i in small_of[n]]
    padded = -(-small.shape[0] // HD) * HD
    small = jnp.pad(small, (0, padded - small.shape[0])).reshape(-1, HD)
    gathered = fetch_small(small).reshape(fsdp, -1).astype(F32)
    tables = []
    offset = 0
    for length in lengths:
        tables.append(gathered[:, offset : offset + length])
        offset += length
    norms, rels = [], []
    for n in range(2):
        own = tables[5 * n : 5 * n + 5]
        norms.append([t.reshape(1, width) for t in own[:4]])
        rels.append(own[4].reshape(HEADS, BUCKETS))
    gates = jax.nn.sigmoid(tables[10].reshape(HEADS))
    gate = lax.dynamic_slice_in_dim(gates, my_head, 1, 0)

    buckets = jnp.asarray(window_buckets())
    mine = [
        jnp.concatenate([lax.dynamic_index_in_dim(rels[n], my_head, 0, keepdims=False), gate])
        for n in range(2)
    ]

    ups = bit_list(fsdp)
    downs = ups[::-1]
    tie = lax.optimization_barrier
    core = (me & 1).reshape(1).astype(jnp.int32)
    shard = width // fsdp
    wide = layers[0][7].shape[1]
    chunks = layers[0][8].shape[0] // shard
    half, half_qkv, half_in = width // 2, 3 * width // 2, wide // 2
    plan_a = [(0, 0, shard, half_qkv, 0, 0), (1, 0, shard, half, 0, half_qkv)]
    plan_b = [(0, 0, shard, half_in, 0, 0)] + [
        (1, n * shard, shard, half, shard, n * half) for n in range(chunks)
    ]

    groups = [
        (n, ids, plan, units * shard)
        for n in range(2)
        for ids, plan, units in (((2, 4), plan_a, 1), ((7, 8), plan_b, 2))
    ]
    packed = []
    for n, ids, plan, count_rows in groups:
        raw = [layers[n][i] for i in ids]
        if packed:
            packed[-1], raw = tie((packed[-1], raw))
        packed.append(pack(raw, plan, count_rows, core))
    gathered = [lax.all_gather(p, "fsdp", axis=0, tiled=False) for p in packed]
    full = [{}, {}]

    def unfold(g, value):
        n, ids, plan, _ = groups[g]
        mine = gathered[g]
        if value is not None:
            value, mine = tie((value, mine))
        for i, w in zip(ids, unfold_weights(mine, [layers[n][i] for i in ids], plan, core)):
            full[n][i] = w
        return value

    unfold(0, None)

    infos = [
        jnp.concatenate([block_slots[m, 0], doc_starts[m, 0]]).astype(jnp.int32) for m in range(micro)
    ]
    rows = memory_rows(mem_keys[0], mem_values[0])
    indices = memory_index(mem_index[:, 0])
    memories = [(rows, *indices[m]) for m in range(micro)]

    state = [inputs[m, 0] for m in range(micro)]
    kept = [[None] * micro, [None] * micro]
    for n in range(2):
        gain_in, bias_in, gain_mid, bias_mid = norms[n]
        w = full[n]
        work = [dict(x=state[m]) for m in range(micro)]
        for m in range(micro):
            work[m]["n1"], pieces = qkv_forward(work[m]["x"], gain_in, bias_in, w[2])
            if m == micro - 1:
                pieces = unfold(1 + 2 * n, pieces)
            work[m]["pieces"] = exchange(pieces)
        for m in range(micro):
            work[m]["saved"], outs = attend(
                work[m]["pieces"], infos[m], mine[n], buckets, memories[m] if n else None
            )
            if n == 0 and m == micro - 1:
                outs = unfold(2, outs)
            work[m]["outs"] = exchange(outs)
        for m in range(micro):
            mixed, hidden, normed_mid, up, act, state[m] = mlp_forward(
                work[m]["x"],
                work[m]["outs"],
                w[4],
                gain_mid,
                bias_mid,
                w[7],
                w[8],
                BF16 if n else F32,
            )
            work[m].update(mixed=mixed, hidden=hidden, n2=normed_mid, up=up, act=act)
        kept[n] = work
    outputs = jnp.stack(state)[:, None]

    lane = Lane()
    smalls = [None, None]
    top = [out_grad[m, 0] for m in range(micro)]
    top_low = top

    def pair(source, name):
        return [item[name] for item in source]

    def launch(key, bits, *what):
        lane.add(key, reduce_steps(*weight_grad(*what, bits=bits), bits))

    def chip_sum(keep, send):
        return add_terms([keep, swap_ctx(send, 1)])

    def shard_sum(x):
        return lax.psum_scatter(x, "fsdp", scatter_dimension=0, tiled=False)

    dims_a = (fsdp, shard, 2 * width)
    dims_b = (fsdp, 2 * shard, half_in)
    sums = {}
    for n in (1, 0):
        gain_in, bias_in, gain_mid, bias_mid = norms[n]
        w = full[n]
        ks = kept[n]
        back = [None] * micro
        for m in range(micro):
            k = ks[m]
            grad = top[m]
            if n == 0 and m == 0:
                grad, sums["b1"], sums["a1"] = tie((grad, sums["b1"], sums["a1"]))
                sums["b1"] = sum_lines(sums["b1"])
                sums["a1"] = shard_sum(sums["a1"])
            du, hb, dh, g_gain_mid, g_bias_mid, pieces = mlp_backward(
                grad, k["up"], w[7], w[8], k["hidden"], gain_mid, w[4]
            )
            back[m] = dict(
                du=du, hb=hb, dh=dh, norms=[g_gain_mid, g_bias_mid], pieces=exchange(pieces)
            )
        act, n2, mixed = pair(ks, "act"), pair(ks, "n2"), pair(ks, "mixed")
        du, hb = pair(back, "du"), pair(back, "hb")
        both = weight_grad(n2, du, shard, width, 0, half_in // width, dims=dims_b)
        both = weight_grad(act, top_low, shard, half, 0, 1, into=both, place=(1, 0), dims=dims_b)
        back[0]["pieces"], both = tie((back[0]["pieces"], both))
        chip = chip_sum(*both)
        for m in range(micro):
            pieces = back[m]["pieces"]
            if m == 1:
                pieces, chip = tie((pieces, chip))
                sums["b%d" % n] = shard_sum(chip)
                if n == 0:
                    pieces, sums["a1"], sums["b1"] = tie((pieces, sums["a1"], sums["b1"]))
                    sums["a1"] = sum_lines(sums["a1"])
            back[m]["extra"], outs = attend_back(
                pieces, infos[m], mine[n], buckets, ks[m]["saved"], memories[m] if n else None
            )
            back[m]["outs"] = exchange(outs)
        for m in range(micro):
            k = ks[m]
            outs = back[m]["outs"]
            if n == 0 and m == 1:
                outs, sums["b0"], sums["a1"] = tie((outs, sums["b0"], sums["a1"]))
                sums["b0"] = sum_lines(sums["b0"])
            dqkv, dx, dx_low, g_gain_in, g_bias_in = qkv_backward(
                k["x"], gain_in, back[m]["dh"], w[2], outs
            )
            back[m].update(dqkv=dqkv, dx=dx, dx_low=dx_low)
            back[m]["norms"] = [g_gain_in, g_bias_in] + back[m]["norms"]
        n1, dqkv = pair(ks, "n1"), pair(back, "dqkv")
        if n:
            both = weight_grad(n1, dqkv, shard, half, 0, 3, dims=dims_a)
            both = weight_grad(mixed, hb, shard, half, 0, 1, into=both, place=(0, 3), dims=dims_a)
            sums["a1"] = chip_sum(*both)
        else:
            launch("out", ups, mixed, hb, shard, half, 0, 1)
            launch("low", ups, n1, dqkv, shard, half_qkv // 2, 0, 1)
            launch("high", downs, n1, dqkv, shard, half_qkv // 2, 1, 1)
        share = HEADS / count
        spot = (jnp.arange(HEADS) == my_head).astype(F32) * share
        rel = jnp.sum(sum(item["extra"][0] for item in back), -1)
        parts = [sum(item["norms"][i] for item in back).reshape(fsdp, -1) for i in range(4)]
        parts.append((spot[:, None] * rel[None, :]).reshape(fsdp, -1))
        if n:
            value = sum(jnp.sum(item["extra"][1]) for item in back) * (gate * (1.0 - gate))[0]
            parts.append((spot * value).reshape(fsdp, -1))
        smalls[n] = parts
        top = pair(back, "dx")
        top_low = pair(back, "dx_low")
    lane.drain()
    dims = [(shard, 3 * width), (shard, width), (shard, wide), (chunks * shard, width)]

    def joined(parts, plan, sizes):
        return merge([p[0] for p in parts], [p[1] for p in parts], plan, sizes, core)

    ready = {key: (value, swap_ctx(value, 1)) for key, value in sums.items()}
    move_b = [(0, 0, shard, half_in, 0, 0, 0, 0, half_in)] + [
        (1, n * shard, shard, half, 0, shard, n * half, 0, half) for n in range(chunks)
    ]
    move_qkv = (0, 0, shard, half_qkv, 0, 0, 0, 0, half_qkv)
    move_out = (1, 0, shard, half, 0, 0, half_qkv, 0, half)
    grads = [{}, {}]
    for n in range(2):
        grads[n][7], grads[n][8] = joined([ready["b%d" % n]], move_b, dims[2:])
    grads[1][2], grads[1][4] = joined([ready["a1"]], [move_qkv, move_out], dims[:2])
    size = half_qkv // 2
    moves = [(0, 0, shard, half_qkv, n, 0, 0, n * size, size) for n in range(2)]
    moves.append((1, 0, shard, half, 2, 0, 0, 0, half))
    done = lane.done
    grads[0][2], grads[0][4] = joined([done["low"], done["high"], done["out"]], moves, dims[:2])

    flat = jnp.concatenate(smalls[0] + smalls[1], 1)
    columns = flat.shape[1]
    flat = jnp.pad(flat, ((0, 0), (0, -columns % HD)))
    for bit in bit_list(count):
        flat = flat + swap_ctx(flat, bit)
    for bit in ups:
        flat = flat + swap_fsdp(flat, bit)
    row = lax.dynamic_index_in_dim(flat, me_fsdp, 0, keepdims=False)
    cuts = []
    offset = 0
    for part in smalls[0] + smalls[1]:
        cuts.append(row[offset : offset + part.shape[1]])
        offset += part.shape[1]
    result = []
    for n in range(2):
        own = cuts[5 * n : 5 * n + 5]
        result += [
            own[0],
            own[1],
            grads[n][2],
            own[4].reshape(-1, BUCKETS),
            grads[n][4],
            own[2],
            own[3],
            grads[n][7],
            grads[n][8],
        ]
    result.append(cuts[10])
    return (outputs, jnp.stack(top)[:, None], *result)


def solution(mesh):
    vector, matrix = P("fsdp"), P("fsdp", None)
    rows = P(None, "fsdp", "ctx", None)
    layer = (vector, vector, matrix, matrix, matrix, vector, vector, matrix, matrix)
    table = P(None, "fsdp", None)
    memory = P("fsdp", "ctx", None)
    return jax.shard_map(
        local,
        mesh=mesh,
        in_specs=(rows, table, table, P(None, "fsdp", "ctx", None, None), memory, memory, rows)
        + layer
        + layer
        + (vector,),
        out_specs=(rows, rows) + layer + layer + (vector,),
        check_vma=False,
    )
```

```python
import functools
import math

import jax
import jax.numpy as jnp
import numpy as np
from jax import lax
from jax.experimental import pallas as pl
from jax.experimental.pallas import tpu as pltpu
from jax.sharding import PartitionSpec as P

HEADS = 8
HD = 128
BUCKETS = 32
WIN = 512
BLK = 128
TOPK = 32
SPAN = WIN + BLK
ROWS = 2 * BLK
LINE = 4
EPS = 1e-05
NEG = -1000000000.0
FAR_DISTANCE = 128
SCALE = HD ** (-0.5)
F32 = jnp.float32
BF16 = jnp.bfloat16
MIB = 1 << 20


def bucket_table(total_count, buckets):
    exact_count = buckets // 2
    result = []
    for distance in range(total_count):
        if distance < exact_count:
            result.append(distance)
        else:
            scaled = math.log(distance / exact_count) / math.log(FAR_DISTANCE / exact_count)
            result.append(min(exact_count + int(scaled * (buckets - exact_count)), buckets - 1))
    return np.array(result, dtype=np.int32)


def window_buckets():
    distance = WIN + np.arange(BLK)[:, None] - np.arange(SPAN)[None, :]
    inside = (distance >= 0) & (distance < WIN)
    buckets = bucket_table(WIN, BUCKETS)[np.clip(distance, 0, WIN - 1)]
    return np.where(inside, buckets, -1).astype(np.int32)


def dot(a, b):
    return lax.dot_general(a, b, (((1,), (0,)), ((), ())), preferred_element_type=F32)


def dot_nt(a, b):
    return lax.dot_general(a, b, (((1,), (1,)), ((), ())), preferred_element_type=F32)


def dot_tn(a, b):
    return lax.dot_general(a, b, (((0,), (0,)), ((), ())), preferred_element_type=F32)


def params(mib):
    return pltpu.CompilerParams(vmem_limit_bytes=mib * MIB)


def cost(flops, nbytes):
    return pl.CostEstimate(flops=int(flops), bytes_accessed=int(nbytes), transcendentals=0)


def vmem():
    return pl.BlockSpec(memory_space=pltpu.VMEM)


def smem():
    return pl.BlockSpec(memory_space=pltpu.SMEM)


def anyspace():
    return pl.BlockSpec(memory_space=pl.ANY)


def shape(dims, kind):
    return jax.ShapeDtypeStruct(tuple(dims), kind)


def whole(dims):
    zeros = (0,) * len(dims)
    return pl.BlockSpec(tuple(dims), lambda *_: zeros)


def single(dims):
    zeros = (0,) * len(dims)
    return pl.BlockSpec(tuple(dims), lambda _: zeros)


def xor_perm(count, bit):
    return [(i, i ^ bit) for i in range(count)]


def bit_list(count):
    bits = []
    bit = 1
    while bit < count:
        bits.append(bit)
        bit *= 2
    return bits


def swap_ctx(x, bit):
    return lax.ppermute(x, "ctx", xor_perm(lax.axis_size("ctx"), bit))


def swap_fsdp(x, bit):
    return lax.ppermute(x, "fsdp", xor_perm(lax.axis_size("fsdp"), bit))


def side_columns(side, half):
    return pl.ds(pl.multiple_of(side * half, HD), half)


def pack_kernel(plan, key, *refs):
    weights, out, held, sems = refs[:-3], refs[-3], refs[-2], refs[-1]
    copies = []
    for n, (i, row, rows, half, to_row, to_column) in enumerate(plan):
        copies.append(
            pltpu.make_async_copy(
                weights[i].at[row : row + rows, side_columns(key[0], half)],
                held.at[to_row : to_row + rows, to_column : to_column + half],
                sems.at[n],
            )
        )
    for copy in copies:
        copy.start()
    for copy in copies:
        copy.wait()
    last = pltpu.make_async_copy(held, out, sems.at[len(plan)])
    last.start()
    last.wait()


def pack(weights, plan, rows, core):
    columns = max(to_column + half for *_, half, _, to_column in plan)
    dims = (rows, columns)
    return pl.pallas_call(
        functools.partial(pack_kernel, plan),
        in_specs=[smem()] + [anyspace()] * len(weights),
        out_specs=anyspace(),
        out_shape=shape(dims, BF16),
        scratch_shapes=[pltpu.VMEM(dims, BF16), pltpu.SemaphoreType.DMA((len(plan) + 1,))],
        compiler_params=params(56),
        cost_estimate=cost(0, 4 * rows * columns),
        name="pack",
    )(core, *weights)


def unfold_kernel(count, plan, shards, key, mine, twin, *refs):
    total = len(shards)
    outs, held, arrive, leave = refs[:total], refs[total : 2 * total], refs[-2], refs[-1]
    groups, n = [], 0
    for i, shard in enumerate(shards):
        for f in range(count):
            copies = []
            for j, row, rows, half, from_row, from_column in plan:
                if j != i:
                    continue
                for ref, side in ((mine, key[0]), (twin, 1 - key[0])):
                    copies.append(
                        pltpu.make_async_copy(
                            ref.at[f, from_row : from_row + rows, from_column : from_column + half],
                            held[i].at[
                                f * shard + row : f * shard + row + rows, side_columns(side, half)
                            ],
                            arrive.at[n],
                        )
                    )
                    n += 1
            span = slice(f * shard, (f + 1) * shard)
            groups.append(
                (copies, pltpu.make_async_copy(held[i].at[span], outs[i].at[span], leave.at[len(groups)]))
            )
    for copies, _ in groups:
        for copy in copies:
            copy.start()
    for copies, last in groups:
        for copy in copies:
            copy.wait()
        last.start()
    for _, last in groups:
        last.wait()


def unfold_weights(mine, twin, weights, plan, core):
    count = lax.axis_size("fsdp")
    shards = [w.shape[0] for w in weights]
    full = [(w.shape[0] * count, w.shape[1]) for w in weights]
    return pl.pallas_call(
        functools.partial(unfold_kernel, count, plan, shards),
        out_shape=[shape(dims, BF16) for dims in full],
        in_specs=[smem(), anyspace(), anyspace()],
        out_specs=[anyspace()] * len(full),
        scratch_shapes=[pltpu.VMEM(dims, BF16) for dims in full]
        + [
            pltpu.SemaphoreType.DMA((2 * count * len(plan),)),
            pltpu.SemaphoreType.DMA((count * len(full),)),
        ],
        compiler_params=params(60),
        cost_estimate=cost(0, 8 * mine.size),
        name="unfold",
    )(core, mine, twin)


def merge(mine, twin, plan, dims, core):
    half = len(mine)

    def body(key, *refs):
        first, second, outs = refs[:half], refs[half : 2 * half], refs[2 * half :]
        for source, side in ((first, key[0]), (second, 1 - key[0])):
            for i, row, rows, width, n, from_row, from_column, offset, size in plan:
                column = pl.multiple_of(side * width + offset, HD)
                outs[i][row : row + rows, pl.ds(column, size)] = source[n][
                    from_row : from_row + rows, from_column : from_column + size
                ].astype(F32)

    return pl.pallas_call(
        body,
        grid=(1,),
        in_specs=[smem()] + [single(x.shape) for x in (*mine, *twin)],
        out_specs=[single(d) for d in dims],
        out_shape=[shape(d, F32) for d in dims],
        compiler_params=params(56),
        cost_estimate=cost(0, sum(8 * a * b for a, b in dims)),
        name="merge",
    )(core, *mine, *twin)


def fetch_small(vector):
    count = lax.axis_size("fsdp")
    have = {0: vector}
    for bit in bit_list(count):
        for r in list(have):
            have[r ^ bit] = swap_fsdp(have[r], bit)
    stacked = jnp.stack([have[r] for r in range(count)])
    return jnp.take(stacked, lax.axis_index("fsdp") ^ jnp.arange(count), axis=0)


def add_terms(terms):
    total = terms[0].astype(F32)
    for term in terms[1:]:
        total = total + term.astype(F32)
    return total.astype(BF16)


def reduce_steps(keep, send, bits):
    count = lax.axis_size("fsdp")
    ctx_count = lax.axis_size("ctx")
    terms = [keep, (yield "ctx", xor_perm(ctx_count, 1), send)]
    left = count
    for bit in bits:
        left //= 2
        got = yield "fsdp", xor_perm(count, bit), add_terms([t[left:] for t in terms])
        terms = [t[:left] for t in terms] + [got]
    return add_terms([t[0] for t in terms])


def lines():
    return [[g for g in range(lax.axis_size("ctx")) if g % 2 == c] for c in range(2)]


def line_steps(mine):
    ctx_count = lax.axis_size("ctx")
    z = (lax.axis_index("ctx") >> 1) & (LINE - 1)
    stride = 2 * LINE

    def along(pairs):
        return [
            (g * stride + 2 * a + c, g * stride + 2 * b + c)
            for g in range(ctx_count // stride)
            for a, b in pairs
            for c in range(2)
        ]

    inner = add_terms([mine, (yield "ctx", along([(0, 1), (3, 2)]), mine)])
    both = add_terms([inner, (yield "ctx", along([(1, 2), (2, 1)]), inner)])
    outer = yield "ctx", along([(1, 0), (2, 3)]), both
    full = jnp.where((z == 0) | (z == LINE - 1), outer, both)
    bit = stride
    while bit < ctx_count:
        full = add_terms([full, (yield "ctx", xor_perm(ctx_count, bit), full)])
        bit *= 2
    return full, (yield "ctx", xor_perm(ctx_count, 1), full)


def all_steps(keep, send, bits):
    return (yield from line_steps((yield from reduce_steps(keep, send, bits))))


class Lane:
    def __init__(self):
        self.active = []
        self.done = {}

    def add(self, key, steps):
        self.active.append((key, steps, next(steps)))

    def advance(self, value=None):
        operands = [request[2] for _, _, request in self.active]
        if value is not None and operands:
            value, operands = lax.optimization_barrier((value, operands))
        left = []
        for (key, steps, (axis, pairs, _)), operand in zip(self.active, operands):
            try:
                left.append((key, steps, steps.send(lax.ppermute(operand, axis, pairs))))
            except StopIteration as stop:
                self.done[key] = stop.value
        self.active = left
        return value

    def drain(self):
        while self.active:
            self.advance()


class Turns:
    def __init__(self):
        self.last = None

    def next(self, value):
        if self.last is not None:
            value, _ = lax.optimization_barrier((value, self.last))
        return value

    def ran(self, value):
        self.last = value
        return value


def grad_kernel(key, a0, a1, k0, k1, s0, s1, *refs):
    keep, send = refs[-2:]
    shard, tile = keep.shape[1], k0.shape[1]
    for n in range(a0.shape[1] // shard):
        left0, left1 = (x[:, n * shard : (n + 1) * shard] for x in (a0, a1))
        span = slice(n * tile, (n + 1) * tile)
        keep[0, :, span] = (dot_tn(left0, k0[...]) + dot_tn(left1, k1[...])).astype(BF16)
        send[0, :, span] = (dot_tn(left0, s0[...]) + dot_tn(left1, s1[...])).astype(BF16)


def shard_order(bits):
    order = [0]
    for bit in reversed(bits):
        order = order + [r | bit for r in order]
    return order


def weight_grad(a, b, shard, tile, first, tiles, bits=None, into=None, place=(0, 0), dims=None):
    count = lax.axis_size("fsdp")
    me = lax.axis_index("fsdp")
    core = lax.axis_index("ctx") & 1
    rows, width = b[0].shape
    across = width // 2 // tile
    chunks = a[0].shape[1] // (count * shard)
    order = jnp.arange(count) if bits is None else me ^ jnp.array(shard_order(bits))
    key = jnp.concatenate([core.reshape(1), order]).astype(jnp.int32)
    dims = dims or (count, shard, chunks * tiles * tile)
    row, column = place
    a_spec = pl.BlockSpec((rows, chunks * shard), lambda t, i, k: (0, k[1 + i]))

    def b_spec(twin):
        return pl.BlockSpec(
            (rows, tile), lambda t, i, k: (0, (1 - k[0] if twin else k[0]) * across + first + t)
        )

    o_spec = pl.BlockSpec((1, shard, chunks * tile), lambda t, i, k: (i, row, column + t))
    extra = list(into or [])
    return pl.pallas_call(
        grad_kernel,
        grid_spec=pltpu.PrefetchScalarGridSpec(
            num_scalar_prefetch=1,
            grid=(tiles, count),
            in_specs=[a_spec, a_spec, b_spec(False), b_spec(False), b_spec(True), b_spec(True)]
            + [anyspace()] * len(extra),
            out_specs=[o_spec, o_spec],
        ),
        out_shape=[shape(dims, BF16)] * 2,
        input_output_aliases={7: 0, 8: 1} if extra else {},
        compiler_params=params(56),
        cost_estimate=cost(
            8 * rows * shard * count * chunks * tiles * tile,
            4 * shard * count * chunks * tiles * tile + 8 * rows * width,
        ),
        name="weight_grad",
    )(key, a[0], a[1], b[0], b[1], b[0], b[1], *extra)


def norm_parts(x):
    centre = x - jnp.mean(x, -1, keepdims=True)
    rstd = lax.rsqrt(jnp.mean(centre * centre, -1, keepdims=True) + EPS)
    return centre * rstd, rstd


def norm_back(x, gain, grad):
    hat, rstd = norm_parts(x)
    scaled = grad * gain
    out = rstd * (
        scaled
        - jnp.mean(scaled, -1, keepdims=True)
        - hat * jnp.mean(scaled * hat, -1, keepdims=True)
    )
    grad_gain = jnp.sum(grad * hat, 0, keepdims=True)
    grad_bias = jnp.sum(grad, 0, keepdims=True)
    return out, grad_gain, grad_bias


GROUP = 4


def qkv_kernel(x_ref, gain, bias, weight, normed, pieces):
    @pl.when(pl.program_id(0) == 0)
    def _():
        hat, _ = norm_parts(x_ref[...].astype(F32))
        normed[...] = (hat * gain[...] + bias[...]).astype(BF16)

    group = dot(normed[...], weight[...]).astype(BF16)
    for copy in range(pieces.shape[0]):
        for h in range(GROUP):
            pieces[copy, h] = group[:, h * HD : (h + 1) * HD]


def qkv_forward(x, gain, bias, weight):
    count = lax.axis_size("ctx")
    width = x.shape[1]
    parts = HEADS // GROUP
    copies = count // HEADS
    normed, pieces = pl.pallas_call(
        qkv_kernel,
        grid=(3 * parts,),
        in_specs=[
            whole(x.shape),
            whole((1, width)),
            whole((1, width)),
            pl.BlockSpec((width, GROUP * HD), lambda t: (0, t)),
        ],
        out_specs=[
            whole((ROWS, width)),
            pl.BlockSpec((copies, GROUP, ROWS, HD), lambda t: (0, t % parts, 0, t // parts)),
        ],
        out_shape=[shape((ROWS, width), BF16), shape((copies, HEADS, ROWS, 3 * HD), BF16)],
        compiler_params=params(56),
        cost_estimate=cost(6 * ROWS * width * width, 8 * width * width),
        name="qkv",
    )(x, gain, bias, weight)
    return normed, pieces.reshape(count, ROWS, 3 * HD)


def gelu(u):
    inner = math.sqrt(2.0 / math.pi) * (u + 0.044715 * u * u * u)
    return 0.5 * u * (1.0 + jnp.tanh(inner))


def gelu_slope(u):
    c = math.sqrt(2.0 / math.pi)
    square = u * u
    t = jnp.tanh(c * (u + 0.044715 * u * square))
    return 0.5 * (1.0 + t) + 0.5 * u * (1.0 - t * t) * (c * (1.0 + 3.0 * 0.044715 * square))


def mlp_kernel(steps, x_ref, w_out, gain, bias, w_in, w_down, pieces, *refs):
    mixed, hidden, normed, up, act, out, total = refs
    step = pl.program_id(0)

    @pl.when(step == 0)
    def _():
        for s in range(HEADS):
            mixed[:, s * HD : (s + 1) * HD] = pieces[s]
        h = x_ref[...].astype(F32) + dot(mixed[...], w_out[...])
        hidden[...] = h
        hat, _ = norm_parts(h)
        normed[...] = (hat * gain[...] + bias[...]).astype(BF16)
        total[...] = h

    u = dot(normed[...], w_in[...])
    up[...] = u.astype(BF16)
    a = gelu(u).astype(BF16)
    act[...] = a
    total[...] += dot(a, w_down[...])

    @pl.when(step == steps - 1)
    def _():
        out[...] = total[...].astype(out.dtype)


def mlp_forward(x, pieces, w_out, gain, bias, w_in, w_down, kind):
    width = x.shape[1]
    ff = w_in.shape[1]
    tile = 512
    steps = ff // tile
    row = (ROWS, width)
    return pl.pallas_call(
        functools.partial(mlp_kernel, steps),
        grid=(steps,),
        in_specs=[
            whole(row),
            whole(w_out.shape),
            whole((1, width)),
            whole((1, width)),
            pl.BlockSpec((width, tile), lambda j: (0, j)),
            pl.BlockSpec((tile, width), lambda j: (j, 0)),
            whole((HEADS, ROWS, HD)),
        ],
        out_specs=[
            whole(row),
            whole(row),
            whole(row),
            pl.BlockSpec((ROWS, tile), lambda j: (0, j)),
            pl.BlockSpec((ROWS, tile), lambda j: (0, j)),
            whole(row),
        ],
        scratch_shapes=[pltpu.VMEM(row, F32)],
        out_shape=[
            shape(row, BF16),
            shape(row, F32),
            shape(row, BF16),
            shape((ROWS, ff), BF16),
            shape((ROWS, ff), BF16),
            shape(row, kind),
        ],
        compiler_params=params(56),
        cost_estimate=cost(2 * ROWS * width * (width + 2 * ff), 2 * width * (width + 2 * ff)),
        name="mlp",
    )(x, w_out, gain, bias, w_in, w_down, pieces)


def mlp_back_kernel(steps, g_ref, up, w_in, w_down, hidden, gain, w_out, *refs):
    du, grad_low, grad_hidden, grad_gain, grad_bias, pieces, total, low = refs
    step = pl.program_id(0)

    @pl.when(step == 0)
    def _():
        low[...] = g_ref[...].astype(BF16)
        total[...] = jnp.zeros_like(total)

    d_act = dot_nt(low[...], w_down[...])
    d_up = (gelu_slope(up[...].astype(F32)) * d_act).astype(BF16)
    du[...] = d_up
    total[...] += dot_nt(d_up, w_in[...])

    @pl.when(step == steps - 1)
    def _():
        part, g_gain, g_bias = norm_back(hidden[...], gain[...], total[...])
        grad_gain[...] = g_gain
        grad_bias[...] = g_bias
        dh = g_ref[...].astype(F32) + part
        grad_hidden[...] = dh
        hb = dh.astype(BF16)
        grad_low[...] = hb
        mixed = dot_nt(hb, w_out[...]).astype(BF16)
        for s in range(pieces.shape[0]):
            h = s % HEADS
            pieces[s] = mixed[:, h * HD : (h + 1) * HD]


def mlp_backward(grad, up, w_in, w_down, hidden, gain, w_out):
    count = lax.axis_size("ctx")
    width = hidden.shape[1]
    ff = w_in.shape[1]
    tile = 512
    steps = ff // tile
    row = (ROWS, width)
    return pl.pallas_call(
        functools.partial(mlp_back_kernel, steps),
        grid=(steps,),
        in_specs=[
            whole(row),
            pl.BlockSpec((ROWS, tile), lambda j: (0, j)),
            pl.BlockSpec((width, tile), lambda j: (0, j)),
            pl.BlockSpec((tile, width), lambda j: (j, 0)),
            whole(row),
            whole((1, width)),
            whole(w_out.shape),
        ],
        out_specs=[
            pl.BlockSpec((ROWS, tile), lambda j: (0, j)),
            whole(row),
            whole(row),
            whole((1, width)),
            whole((1, width)),
            whole((count, ROWS, HD)),
        ],
        scratch_shapes=[pltpu.VMEM(row, F32), pltpu.VMEM(row, BF16)],
        out_shape=[
            shape((ROWS, ff), BF16),
            shape(row, BF16),
            shape(row, F32),
            shape((1, width), F32),
            shape((1, width), F32),
            shape((count, ROWS, HD), BF16),
        ],
        compiler_params=params(56),
        cost_estimate=cost(2 * ROWS * width * (width + 2 * ff), 2 * width * (width + 2 * ff)),
        name="mlp_back",
    )(grad, up, w_in, w_down, hidden, gain, w_out)


def qkv_back_kernel(x_ref, gain, grad_hidden, weight, pieces, *refs):
    dqkv, grad_x, grad_low, grad_gain, grad_bias, total = refs
    step = pl.program_id(0)

    @pl.when(step == 0)
    def _():
        total[...] = jnp.zeros_like(total)

    for h in range(GROUP):
        dqkv[:, h * HD : (h + 1) * HD] = pieces[h]
    total[...] += dot_nt(dqkv[...], weight[...])

    @pl.when(step == pl.num_programs(0) - 1)
    def _():
        part, g_gain, g_bias = norm_back(x_ref[...].astype(F32), gain[...], total[...])
        grad_gain[...] = g_gain
        grad_bias[...] = g_bias
        result = grad_hidden[...] + part
        grad_x[...] = result
        grad_low[...] = result.astype(BF16)


def qkv_backward(x, gain, grad_hidden, weight, pieces):
    width = x.shape[1]
    row = (ROWS, width)
    parts = HEADS // GROUP
    wide = GROUP * HD
    return pl.pallas_call(
        qkv_back_kernel,
        grid=(3 * parts,),
        in_specs=[
            whole(row),
            whole((1, width)),
            whole(row),
            pl.BlockSpec((width, wide), lambda t: (0, t)),
            pl.BlockSpec((GROUP, ROWS, HD), lambda t: (t % parts, 0, t // parts)),
        ],
        out_specs=[
            pl.BlockSpec((ROWS, wide), lambda t: (0, t)),
            whole(row),
            whole(row),
            whole((1, width)),
            whole((1, width)),
        ],
        scratch_shapes=[pltpu.VMEM(row, F32)],
        out_shape=[
            shape((ROWS, 3 * width), BF16),
            shape(row, F32),
            shape(row, BF16),
            shape((1, width), F32),
            shape((1, width), F32),
        ],
        compiler_params=params(56),
        cost_estimate=cost(6 * ROWS * width * width, 6 * width * width),
        name="qkv_back",
    )(x, gain, grad_hidden, weight, pieces)


CHUNK = 64


def pick_scores(score_ref, index_ref, base, chunk):
    parts = []
    for r in range(CHUNK // 8):
        at = chunk * CHUNK + r * 8
        rows = pl.ds(pl.multiple_of(at, 8), 8)
        index = index_ref[pl.ds(pl.multiple_of(base + at, 8), 8), :]
        low = index & (HD - 1)
        high = index >> 7
        found = jnp.zeros((8, HD), F32)
        for tile in range(score_ref.shape[1] // HD):
            part = jnp.take_along_axis(
                score_ref[rows, tile * HD : (tile + 1) * HD], low, axis=1, mode="promise_in_bounds"
            )
            found = jnp.where(high == tile, part, found)
        parts.append(found)
    return jnp.concatenate(parts, 0)


def scatter_rows(value_ref, value_base, index_ref, flat_ref, base, dense_ref, group):
    high_count = dense_ref.shape[1] // HD
    row = lax.broadcasted_iota(jnp.int32, (16, HD), 0) & 7
    lane = lax.broadcasted_iota(jnp.int32, (16, HD), 1) >> 5
    masks = [(row == lane + 4 * u).astype(F32).astype(BF16) for u in range(2)]
    place = lax.broadcasted_iota(jnp.int32, (HD, HD), 0).astype(F32).astype(BF16)
    zero, one, none = jnp.zeros((16, HD), BF16), jnp.ones((HD, HD), BF16), jnp.zeros((HD, HD), BF16)
    found = []
    for g in range(2):
        at = group * 16 + g * 8
        value = value_ref[pl.ds(pl.multiple_of(value_base + at, 8), 8), :]
        high = (index_ref[pl.ds(pl.multiple_of(base + at, 8), 8), :] >> 7).astype(F32)
        value = jnp.concatenate([value, value], 0).astype(BF16)
        high = jnp.concatenate([high, high - 1.0], 0).astype(BF16)
        spots = [value * mask for mask in masks]
        bands = []
        for h in range(0, high_count, 2):
            hit = high == jnp.array(h, BF16)
            bands.append(jnp.concatenate([jnp.where(hit, spot, zero) for spot in spots], 1))
        left = jnp.concatenate(bands, 0)
        columns = []
        for u in range(2):
            flat = flat_ref[pl.ds((base + at) // 4 + u, 1), :]
            flat = jnp.broadcast_to(flat, (16, HD)).astype(BF16)
            flat = jnp.concatenate([flat] * (HD // 16), 0)
            columns.append(jnp.where(place == flat, one, none))
        found.append(dot_nt(left, jnp.concatenate(columns, 1)))
    rows = pl.ds(pl.multiple_of(group * 16, 16), 16)
    for h in range(high_count):
        both = [f[h * 8 : (h + 1) * 8, :] for f in found]
        dense_ref[rows, h * HD : (h + 1) * HD] = jnp.concatenate(both, 0).astype(BF16)


def attend_kernel(recall, count, info, rel, buckets, pieces, *refs):
    if recall:
        mem, index, flat = refs[:3]
        refs = refs[3:]
    queries, keys, values, probs, outs = refs[:5]
    refs = refs[5:]
    if recall:
        weights, gap, mixed, bias, scores, dense = refs
    else:
        mixed, bias = refs

    def table(n, carry):
        rows = pl.ds(pl.multiple_of(n * 8, 8), 8)
        bucket = buckets[rows, :]
        part = jnp.full(bucket.shape, NEG, F32)
        for b in range(BUCKETS):
            part = jnp.where(bucket == b, rel[b], part)
        bias[rows, :] = part
        return carry

    lax.fori_loop(0, BLK // 8, table, 0)
    keys[0:WIN, :] = jnp.zeros((WIN, HD), BF16)
    values[0:WIN, :] = jnp.zeros((WIN, HD), BF16)
    for s in range(count):
        queries[s * ROWS : (s + 1) * ROWS, :] = pieces[s, :, :HD]
        for half in range(2):
            row = pl.multiple_of(info[2 * s + half] * BLK + WIN, BLK)
            span = slice(half * BLK, (half + 1) * BLK)
            keys[pl.ds(row, BLK), :] = pieces[s, span, HD : 2 * HD]
            values[pl.ds(row, BLK), :] = pieces[s, span, 2 * HD :]

    def one(s, carry):
        base = pl.multiple_of(s * ROWS, ROWS)
        for half in range(2):
            block = info[2 * s + half]
            row = pl.multiple_of(block * BLK, BLK)
            mine = pl.ds(pl.multiple_of(base + half * BLK, BLK), BLK)
            score = dot_nt(queries[mine, :], keys[pl.ds(row, SPAN), :]) * SCALE + bias[...]
            at = row + lax.broadcasted_iota(jnp.int32, (BLK, 1), 0)
            begin = jnp.zeros((BLK, 1), jnp.int32)
            for d in range(4):
                start = info[2 * count + d]
                begin = jnp.where(at >= start, jnp.maximum(begin, start), begin)
            key_at = row - WIN + lax.broadcasted_iota(jnp.int32, (1, SPAN), 1)
            score = jnp.where(key_at >= begin, score, NEG)
            exps = jnp.exp(score - jnp.max(score, -1, keepdims=True))
            prob = (exps * (1.0 / jnp.sum(exps, -1, keepdims=True))).astype(BF16)
            probs[2 * s + half] = prob
            mixed[mine, :] = dot(prob, values[pl.ds(row, SPAN), :])
        if recall:
            tile = pl.ds(base, ROWS)
            scores[...] = dot_nt(queries[tile, :], mem[:, :HD])

            def choose(chunk, inner):
                found = pick_scores(scores, index, base, chunk) * SCALE
                exps = jnp.exp(found - jnp.max(found, -1, keepdims=True))
                weight = exps * ((HD // TOPK) / jnp.sum(exps, -1, keepdims=True))
                weights[pl.ds(pl.multiple_of(base + chunk * CHUNK, CHUNK), CHUNK), :] = weight
                return inner

            lax.fori_loop(0, ROWS // CHUNK, choose, 0, unroll=4)

            def place(group, inner):
                scatter_rows(weights, base, index, flat, base, dense, group)
                return inner

            lax.fori_loop(0, ROWS // 16, place, 0, unroll=16)
            found = dot(dense[...], mem[:, HD:])
            near = mixed[tile, :]
            gap[tile, :] = found - near
            gate = rel[BUCKETS]
            mixed[tile, :] = gate * found + (1.0 - gate) * near
        return carry

    lax.fori_loop(0, count, one, 0)
    for s in range(count):
        outs[s] = mixed[s * ROWS : (s + 1) * ROWS, :].astype(BF16)


def attend(pieces, info, rel, buckets, memory):
    count = lax.axis_size("ctx")
    total = count * ROWS
    recall = memory is not None
    operands = [info, rel, buckets, pieces]
    outs = [
        shape((total, HD), BF16),
        shape((total + WIN, HD), BF16),
        shape((total + WIN, HD), BF16),
        shape((2 * count, BLK, SPAN), BF16),
        shape((count, ROWS, HD), BF16),
    ]
    scratch = [pltpu.VMEM((total, HD), F32), pltpu.VMEM((BLK, SPAN), F32)]
    if recall:
        operands += list(memory)
        outs += [shape((total, HD), F32), shape((total, HD), F32)]
        rows = memory[0].shape[0]
        scratch += [pltpu.VMEM((ROWS, rows), F32), pltpu.VMEM((ROWS, rows), BF16)]
    result = pl.pallas_call(
        functools.partial(attend_kernel, recall, count),
        grid=(1,),
        in_specs=[smem(), smem()] + [single(x.shape) for x in operands[2:]],
        out_specs=[single(x.shape) for x in outs],
        out_shape=outs,
        scratch_shapes=scratch,
        compiler_params=params(60),
        cost_estimate=cost(45e9 if recall else 12e9, 8e6),
        name="recall_attend" if recall else "local_attend",
    )(*operands)
    return list(result[:4]) + list(result[5:]), result[4]


def attend_back_kernel(recall, count, info, rel, buckets, pieces, *refs):
    queries, keys, values, probs = refs[:4]
    refs = refs[4:]
    if recall:
        weights, gap, mem, index, flat, grad_rel, gate_sum = refs[:7]
        refs = refs[7:]
    else:
        grad_rel, refs = refs[0], refs[1:]
    outs, spread_sum, grads, dq, dk, dv = refs[:6]
    if recall:
        scores, dense, picked, mem_low = refs[6:]
        gate_sum[...] = jnp.zeros_like(gate_sum)
        gate = rel[BUCKETS]

    for s in range(count):
        grads[s * ROWS : (s + 1) * ROWS, :] = pieces[s]
    dk[...] = jnp.zeros_like(dk)
    dv[...] = jnp.zeros_like(dv)
    spread_sum[...] = jnp.zeros_like(spread_sum)

    def one(s, carry):
        base = pl.multiple_of(s * ROWS, ROWS)
        for half in range(2):
            block = info[2 * s + half]
            row = pl.multiple_of(block * BLK, BLK)
            mine = pl.ds(pl.multiple_of(base + half * BLK, BLK), BLK)
            near = pl.ds(row, SPAN)
            grad = grads[mine, :]
            if recall:
                grad = ((1.0 - gate) * grad.astype(F32)).astype(BF16)
            prob_low = probs[2 * s + half]
            prob = prob_low.astype(F32)
            d_prob = dot_nt(grad, values[near, :])
            product = prob * d_prob
            d_score = product - prob * jnp.sum(product, -1, keepdims=True)
            spread_sum[...] += d_score
            low = d_score.astype(BF16)
            dq[mine, :] = dot(low, keys[near, :]) * SCALE
            dk[near, :] += dot_tn(low, queries[mine, :]) * SCALE
            dv[near, :] += dot_tn(prob_low, grad)
        if recall:
            tile = pl.ds(base, ROWS)
            grad = grads[tile, :].astype(F32)
            gate_sum[...] += jnp.sum((grad * gap[tile, :]).reshape(ROWS // 8, 8, HD), 0)
            mem_low[...] = (gate * grad).astype(BF16)
            scores[...] = dot_nt(mem_low[...], mem[:, HD:])

            def choose(chunk, inner):
                found = pick_scores(scores, index, base, chunk)
                rows = pl.ds(pl.multiple_of(base + chunk * CHUNK, CHUNK), CHUNK)
                weight = weights[rows, :]
                product = weight * found
                centre = jnp.sum(product, -1, keepdims=True) * (TOPK / HD)
                local_rows = pl.ds(pl.multiple_of(chunk * CHUNK, CHUNK), CHUNK)
                picked[local_rows, :] = product - weight * centre
                return inner

            lax.fori_loop(0, ROWS // CHUNK, choose, 0, unroll=4)

            def place(group, inner):
                scatter_rows(picked, 0, index, flat, base, dense, group)
                return inner

            lax.fori_loop(0, ROWS // 16, place, 0, unroll=16)
            dq[tile, :] += dot(dense[...], mem[:, :HD]) * SCALE
        return carry

    lax.fori_loop(0, count, one, 0)
    for b in range(BUCKETS):
        part = jnp.sum(jnp.where(buckets[...] == b, spread_sum[...], 0.0), 0, keepdims=True)
        line = part[:, :HD]
        for n in range(1, SPAN // HD):
            line = line + part[:, n * HD : (n + 1) * HD]
        grad_rel[b : b + 1, :] = line
    for s in range(count):
        outs[s, :, :HD] = dq[s * ROWS : (s + 1) * ROWS, :].astype(BF16)
        for half in range(2):
            row = pl.multiple_of(info[2 * s + half] * BLK + WIN, BLK)
            span = slice(half * BLK, (half + 1) * BLK)
            outs[s, span, HD : 2 * HD] = dk[pl.ds(row, BLK), :].astype(BF16)
            outs[s, span, 2 * HD :] = dv[pl.ds(row, BLK), :].astype(BF16)


def attend_back(pieces, info, rel, buckets, saved, memory):
    count = lax.axis_size("ctx")
    total = count * ROWS
    recall = memory is not None
    operands = [info, rel, buckets, pieces, *saved]
    outs = [shape((BUCKETS, HD), F32)]
    scratch = [
        pltpu.VMEM((BLK, SPAN), F32),
        pltpu.VMEM((total, HD), BF16),
        pltpu.VMEM((total, HD), F32),
        pltpu.VMEM((total + WIN, HD), F32),
        pltpu.VMEM((total + WIN, HD), F32),
    ]
    if recall:
        operands += list(memory)
        rows = memory[0].shape[0]
        outs += [shape((8, HD), F32)]
        scratch += [
            pltpu.VMEM((ROWS, rows), F32),
            pltpu.VMEM((ROWS, rows), BF16),
            pltpu.VMEM((ROWS, HD), F32),
            pltpu.VMEM((ROWS, HD), BF16),
        ]
    outs += [shape((count, ROWS, 3 * HD), BF16)]
    result = pl.pallas_call(
        functools.partial(attend_back_kernel, recall, count),
        grid=(1,),
        in_specs=[smem(), smem()] + [single(x.shape) for x in operands[2:]],
        out_specs=[single(x.shape) for x in outs],
        out_shape=outs,
        scratch_shapes=scratch,
        compiler_params=params(60),
        cost_estimate=cost(50e9 if recall else 20e9, 8e6),
        name="recall_back" if recall else "local_back",
    )(*operands)
    return list(result[:-1]), result[-1]


def memory_rows(keys, values, exchange):
    count = lax.axis_size("ctx")

    def pieces(array):
        return [array[:, h * HD : (h + 1) * HD] for h in range(HEADS)]

    both = [jnp.concatenate(pair, 1) for pair in zip(pieces(keys), pieces(values))]
    stacked = jnp.stack(both * (count // HEADS))
    return exchange(stacked).reshape(count * ROWS, 2 * HD)


def memory_index(mem_index, exchange):
    count = lax.axis_size("ctx")
    micro = mem_index.shape[0]
    by_head = jnp.transpose(mem_index, (2, 0, 1, 3)).reshape(HEADS, micro, ROWS * TOPK // HD, HD)
    got = exchange(jnp.concatenate([by_head] * (count // HEADS), 0))
    result = []
    for m in range(micro):
        flat = got[:, m].reshape(-1, HD)
        index = jnp.tile(flat.reshape(count * ROWS, TOPK), (1, HD // TOPK))
        result.append((index, (flat & (HD - 1)).astype(F32)))
    return result


def local(
    inputs,
    block_slots,
    doc_starts,
    mem_index,
    mem_keys,
    mem_values,
    out_grad,
    *weights,
):
    me = lax.axis_index("ctx")
    me_fsdp = lax.axis_index("fsdp")
    count = lax.axis_size("ctx")
    fsdp = lax.axis_size("fsdp")
    micro = inputs.shape[0]
    width = inputs.shape[-1]
    my_head = me & (HEADS - 1)

    layers = [list(weights[:9]), list(weights[9:19])]
    small_of = [[0, 1, 5, 6, 3], [0, 1, 5, 6, 3, 9]]
    small = jnp.concatenate(
        [layers[n][i].reshape(-1) for n in range(2) for i in small_of[n]]
    )
    lengths = [layers[n][i].size for n in range(2) for i in small_of[n]]
    padded = -(-small.shape[0] // HD) * HD
    small = jnp.pad(small, (0, padded - small.shape[0])).reshape(-1, HD)
    gathered = fetch_small(small).reshape(fsdp, -1).astype(F32)
    tables = []
    offset = 0
    for length in lengths:
        tables.append(gathered[:, offset : offset + length])
        offset += length
    norms, rels = [], []
    for n in range(2):
        own = tables[5 * n : 5 * n + 5]
        norms.append([t.reshape(1, width) for t in own[:4]])
        rels.append(own[4].reshape(HEADS, BUCKETS))
    gates = jax.nn.sigmoid(tables[10].reshape(HEADS))
    gate = lax.dynamic_slice_in_dim(gates, my_head, 1, 0)

    buckets = jnp.asarray(window_buckets())
    mine = [
        jnp.concatenate([lax.dynamic_index_in_dim(rels[n], my_head, 0, keepdims=False), gate])
        for n in range(2)
    ]

    ups = bit_list(fsdp)
    downs = ups[::-1]
    tie = lax.optimization_barrier
    core = (me & 1).reshape(1).astype(jnp.int32)
    shard = width // fsdp
    wide = layers[0][7].shape[1]
    chunks = layers[0][8].shape[0] // shard
    half, half_qkv, half_in = width // 2, 3 * width // 2, wide // 2
    quarter = shard // 4
    down = [(n * shard, shard, half, n * half) for n in range(chunks)]
    groups = [
        ([(0, 2)], [(0, 0, shard, half_qkv, 0, 0)], shard),
        (
            [(0, 4), (1, 2), (0, 7), (0, 8)],
            [
                (0, 0, shard, half, 0, 0),
                (1, 0, shard, half_qkv, 0, half),
                (2, 0, shard, half_in, shard, 0),
            ]
            + [(3, row, rows, wide_half, 2 * shard, col) for row, rows, wide_half, col in down],
            3 * shard,
        ),
        (
            [(1, 7), (1, 8), (1, 4)],
            [(0, 0, shard, half_in, 0, 0)]
            + [(1, row, rows, wide_half, shard, col) for row, rows, wide_half, col in down]
            + [(2, n * quarter, quarter, half, 2 * shard, n * half) for n in range(4)],
            2 * shard + quarter,
        ),
    ]
    packed = []
    for ids, plan, count_rows in groups:
        raw = [layers[n][i] for n, i in ids]
        if packed:
            packed[-1], raw = tie((packed[-1], raw))
        packed.append(pack(raw, plan, count_rows, core))
    gathered = [lax.all_gather(p, "fsdp", axis=0, tiled=False) for p in packed]
    full = [{}, {}]

    twins = {}
    turns = Turns()

    def hand_over(g, value):
        value, gathered[g] = tie((value, gathered[g]))
        twins[g] = swap_ctx(gathered[g], 1)
        return value

    def unfold(g):
        ids, plan, _ = groups[g]
        raw = [layers[n][i] for n, i in ids]
        result = unfold_weights(turns.next(gathered[g]), twins[g], raw, plan, core)
        for (n, i), w in zip(ids, result):
            full[n][i] = w
        turns.ran(result[0])


    infos = [
        jnp.concatenate([block_slots[m, 0], doc_starts[m, 0]]).astype(jnp.int32) for m in range(micro)
    ]
    links = Turns()

    def exchange(x):
        return links.ran(lax.all_to_all(links.next(x), "ctx", 0, 0, tiled=False))

    rows = memory_rows(mem_keys[0], mem_values[0], exchange)
    indices = memory_index(mem_index[:, 0], exchange)
    hand_over(0, links.last)
    unfold(0)
    memories = [(rows, *indices[m]) for m in range(micro)]

    state = [inputs[m, 0] for m in range(micro)]
    kept = [None, None]
    projected = [{} for _ in range(micro)]
    for n in range(2):
        gain_in, bias_in, gain_mid, bias_mid = norms[n]
        w = full[n]
        work = [dict(x=state[m]) for m in range(micro)]

        def project(m):
            work[m]["n1"], pieces = qkv_forward(turns.next(work[m]["x"]), gain_in, bias_in, w[2])
            work[m]["pieces"] = exchange(turns.ran(pieces))

        if n == 0:
            for m in range(micro):
                project(m)
        for m in range(micro):
            pieces = turns.next(projected[m]["pieces"] if n else work[m]["pieces"])
            if m == micro - 1:
                pieces = hand_over(1 + n, pieces)
            work[m]["saved"], outs = attend(
                pieces, infos[m], mine[n], buckets, memories[m] if n else None
            )
            work[m]["outs"] = exchange(turns.ran(outs))
        unfold(1 + n)
        for m in range(micro):
            outs = turns.next(work[m]["outs"])
            mixed, hidden, normed_mid, up, act, state[m] = mlp_forward(
                work[m]["x"],
                outs,
                w[4],
                gain_mid,
                bias_mid,
                w[7],
                w[8],
                BF16 if n else F32,
            )
            turns.ran(act)
            work[m].update(mixed=mixed, hidden=hidden, n2=normed_mid, up=up, act=act)
            if n == 0:
                gain, bias = norms[1][:2]
                projected[m]["n1"], pieces = qkv_forward(
                    turns.next(state[m]), gain, bias, full[1][2]
                )
                projected[m]["pieces"] = exchange(turns.ran(pieces))
        if n:
            for m in range(micro):
                work[m]["n1"] = projected[m]["n1"]
        kept[n] = work
    outputs = jnp.stack(state)[:, None]

    lane = Lane()
    smalls = [None, None]

    def pair(source, name):
        return [item[name] for item in source]

    def grad_pair(a, *rest, bits=None, **more):
        both = weight_grad([turns.next(a[0]), *a[1:]], *rest, bits=bits, **more)
        return turns.ran(both)

    def launch(key, bits, *what):
        lane.add(key, reduce_steps(*grad_pair(*what, bits=bits), bits))

    def shard_sum(x):
        return lax.psum_scatter(x, "fsdp", scatter_dimension=0, tiled=False)

    def dense_back(n, m, grad):
        k = kept[n][m]
        w = full[n]
        du, hb, dh, g_gain, g_bias, pieces = mlp_backward(
            turns.next(grad), k["up"], w[7], w[8], k["hidden"], norms[n][2], w[4]
        )
        turns.ran(pieces)
        back[n][m].update(
            du=du, hb=hb, dh=dh, norms=[g_gain, g_bias], pieces=exchange(pieces)
        )

    def heads_back(n, m, pieces):
        item = back[n][m]
        item["extra"], outs = attend_back(
            turns.next(pieces), infos[m], mine[n], buckets, kept[n][m]["saved"],
            memories[m] if n else None,
        )
        item["outs"] = exchange(turns.ran(outs))

    def input_back(n, m, outs):
        k, item = kept[n][m], back[n][m]
        dqkv, dx, dx_low, g_gain, g_bias = qkv_backward(
            k["x"], norms[n][0], item["dh"], full[n][2], turns.next(outs)
        )
        turns.ran(dqkv)
        item.update(dqkv=dqkv, dx=dx, dx_low=dx_low)
        item["norms"] = [g_gain, g_bias] + item["norms"]

    def grad_b(n, top_low):
        ks, items = kept[n], back[n]
        both = grad_pair(
            pair(ks, "n2"), pair(items, "du"), shard, width, 0, half_in // width, dims=dims_b
        )
        return grad_pair(
            pair(ks, "act"), top_low, shard, half, 0, 1, into=both, place=(1, 0), dims=dims_b
        )

    back = [[{} for _ in range(micro)] for _ in range(2)]
    dims_a = (fsdp, shard, 2 * width)
    dims_b = (fsdp, 2 * shard, half_in)
    top = [out_grad[m, 0] for m in range(micro)]
    for m in range(micro):
        dense_back(1, m, top[m])
    keep_b, send_b = grad_b(1, top)
    pieces, send_b = tie((back[1][0]["pieces"], send_b))
    got_b = swap_ctx(send_b, 1)
    heads_back(1, 0, pieces)
    pieces, chip = tie((back[1][1]["pieces"], add_terms([keep_b, turns.next(got_b)])))
    sum_b = shard_sum(chip)
    heads_back(1, 1, pieces)
    both = grad_pair(
        pair(kept[1], "mixed"), pair(back[1], "hb"), shard, half, 0, 1, place=(0, 3), dims=dims_a
    )
    for m in range(micro):
        outs = back[1][m]["outs"]
        if m == 1:
            outs, sum_b = tie((outs, sum_b))
            full_b = lax.psum(sum_b, "ctx", axis_index_groups=lines())
        input_back(1, m, outs)
        dense_back(0, m, back[1][m]["dx"])
    heads_back(0, 0, back[0][0]["pieces"])
    for key, bits, left, right, tile in (
        ("in0", ups, pair(kept[0], "n2"), pair(back[0], "du"), width),
        ("down0", downs, pair(kept[0], "act"), pair(back[1], "dx_low"), half),
    ):
        tiles = right[0].shape[1] // 2 // tile
        both_0 = grad_pair(left, right, shard, tile, 0, tiles, bits=bits)
        lane.add(key, all_steps(*both_0, bits))
    heads_back(0, 1, lane.advance(back[0][1]["pieces"]))
    keep_a, send_a = grad_pair(
        pair(kept[1], "n1"), pair(back[1], "dqkv"), shard, half_qkv, 0, 1, into=both, dims=dims_a
    )
    got_a = swap_ctx(send_a, 1)
    input_back(0, 0, lane.advance(back[0][0]["outs"]))
    outs, chip = tie((back[0][1]["outs"], add_terms([keep_a, turns.next(got_a)])))
    sum_a = shard_sum(chip)
    input_back(0, 1, lane.advance(outs))
    n1, dqkv = pair(kept[0], "n1"), pair(back[0], "dqkv")
    launch("low", ups, n1, dqkv, shard, half_qkv // 2, 0, 1)
    launch("high", downs, n1, dqkv, shard, half_qkv // 2, 1, 1)
    launch("out", ups, pair(kept[0], "mixed"), pair(back[0], "hb"), shard, half, 0, 1)
    full_b = turns.next(full_b)
    lane.done["b1"] = full_b, swap_ctx(full_b, 1)
    lane.add("a1", line_steps(sum_a))
    top = pair(back[0], "dx")
    for n in range(2):
        items = back[n]
        share = HEADS / count
        spot = (jnp.arange(HEADS) == my_head).astype(F32) * share
        rel = jnp.sum(sum(item["extra"][0] for item in items), -1)
        parts = [sum(item["norms"][i] for item in items).reshape(fsdp, -1) for i in range(4)]
        parts.append((spot[:, None] * rel[None, :]).reshape(fsdp, -1))
        if n:
            value = sum(jnp.sum(item["extra"][1]) for item in items) * (gate * (1.0 - gate))[0]
            parts.append((spot * value).reshape(fsdp, -1))
        smalls[n] = parts
    lane.drain()
    last = jnp.concatenate([lane.done[key] for key in ("low", "high", "out")], 1)
    for n in range(2):
        lane.add("a0%d" % n, line_steps(last[n * (shard // 2) : (n + 1) * (shard // 2)]))
    lane.drain()
    dims = [(shard, 3 * width), (shard, width), (shard, wide), (chunks * shard, width)]

    def joined(parts, plan, sizes):
        return merge([p[0] for p in parts], [p[1] for p in parts], plan, sizes, core)

    done = lane.done
    move_in = (0, 0, shard, half_in, 0, 0, 0, 0, half_in)
    move_qkv = (0, 0, shard, half_qkv, 0, 0, 0, 0, half_qkv)
    move_out = (1, 0, shard, half, 0, 0, half_qkv, 0, half)

    def move_down(n, row):
        return [(1, i * shard, shard, half, n, row, i * half, 0, half) for i in range(chunks)]

    grads = [{}, {}]
    grads[1][7], grads[1][8] = joined([done["b1"]], [move_in] + move_down(0, shard), dims[2:])
    parts = [done["in0"], done["down0"]]
    grads[0][7], grads[0][8] = joined(parts, [move_in] + move_down(1, 0), dims[2:])
    grads[1][2], grads[1][4] = joined([done["a1"]], [move_qkv, move_out], dims[:2])
    mid = shard // 2
    moves = [
        (i, n * mid, mid, wide_half, n, 0, col, 0, wide_half)
        for n in range(2)
        for i, wide_half, col in ((0, half_qkv, 0), (1, half, half_qkv))
    ]
    grads[0][2], grads[0][4] = joined([done["a00"], done["a01"]], moves, dims[:2])

    flat = jnp.concatenate(smalls[0] + smalls[1], 1)
    columns = flat.shape[1]
    flat = jnp.pad(flat, ((0, 0), (0, -columns % HD)))
    for bit in bit_list(count):
        flat = flat + swap_ctx(flat, bit)
    for bit in ups:
        flat = flat + swap_fsdp(flat, bit)
    row = lax.dynamic_index_in_dim(flat, me_fsdp, 0, keepdims=False)
    cuts = []
    offset = 0
    for part in smalls[0] + smalls[1]:
        cuts.append(row[offset : offset + part.shape[1]])
        offset += part.shape[1]
    result = []
    for n in range(2):
        own = cuts[5 * n : 5 * n + 5]
        result += [
            own[0],
            own[1],
            grads[n][2],
            own[4].reshape(-1, BUCKETS),
            grads[n][4],
            own[2],
            own[3],
            grads[n][7],
            grads[n][8],
        ]
    result.append(cuts[10])
    return (outputs, jnp.stack(top)[:, None], *result)


def solution(mesh):
    vector, matrix = P("fsdp"), P("fsdp", None)
    rows = P(None, "fsdp", "ctx", None)
    layer = (vector, vector, matrix, matrix, matrix, vector, vector, matrix, matrix)
    table = P(None, "fsdp", None)
    memory = P("fsdp", "ctx", None)
    return jax.shard_map(
        local,
        mesh=mesh,
        in_specs=(rows, table, table, P(None, "fsdp", "ctx", None, None), memory, memory, rows)
        + layer
        + layer
        + (vector,),
        out_specs=(rows, rows) + layer + layer + (vector,),
        check_vma=False,
    )
```

```python
import functools
import math

import jax
import jax.numpy as jnp
import numpy as np
from jax import lax
from jax.experimental import pallas as pl
from jax.experimental.pallas import tpu as pltpu
from jax.sharding import PartitionSpec as P

HEADS = 8
HD = 128
BUCKETS = 32
WIN = 512
BLK = 128
TOPK = 32
SPAN = WIN + BLK
ROWS = 2 * BLK
LINE = 4
EPS = 1e-05
NEG = -1000000000.0
FAR_DISTANCE = 128
SCALE = HD ** (-0.5)
F32 = jnp.float32
BF16 = jnp.bfloat16
MIB = 1 << 20


def bucket_table(total_count, buckets):
    exact_count = buckets // 2
    result = []
    for distance in range(total_count):
        if distance < exact_count:
            result.append(distance)
        else:
            scaled = math.log(distance / exact_count) / math.log(FAR_DISTANCE / exact_count)
            result.append(min(exact_count + int(scaled * (buckets - exact_count)), buckets - 1))
    return np.array(result, dtype=np.int32)


def window_buckets():
    distance = WIN + np.arange(BLK)[:, None] - np.arange(SPAN)[None, :]
    inside = (distance >= 0) & (distance < WIN)
    buckets = bucket_table(WIN, BUCKETS)[np.clip(distance, 0, WIN - 1)]
    return np.where(inside, buckets, -1).astype(np.int32)


def dot(a, b):
    return lax.dot_general(a, b, (((1,), (0,)), ((), ())), preferred_element_type=F32)


def dot_nt(a, b):
    return lax.dot_general(a, b, (((1,), (1,)), ((), ())), preferred_element_type=F32)


def dot_tn(a, b):
    return lax.dot_general(a, b, (((0,), (0,)), ((), ())), preferred_element_type=F32)


def params(mib):
    return pltpu.CompilerParams(vmem_limit_bytes=mib * MIB)


def cost(flops, nbytes):
    return pl.CostEstimate(flops=int(flops), bytes_accessed=int(nbytes), transcendentals=0)


def vmem():
    return pl.BlockSpec(memory_space=pltpu.VMEM)


def smem():
    return pl.BlockSpec(memory_space=pltpu.SMEM)


def anyspace():
    return pl.BlockSpec(memory_space=pl.ANY)


def shape(dims, kind):
    return jax.ShapeDtypeStruct(tuple(dims), kind)


def whole(dims):
    zeros = (0,) * len(dims)
    return pl.BlockSpec(tuple(dims), lambda *_: zeros)


def single(dims):
    zeros = (0,) * len(dims)
    return pl.BlockSpec(tuple(dims), lambda _: zeros)


def xor_perm(count, bit):
    return [(i, i ^ bit) for i in range(count)]


def bit_list(count):
    bits = []
    bit = 1
    while bit < count:
        bits.append(bit)
        bit *= 2
    return bits


def swap_ctx(x, bit):
    return lax.ppermute(x, "ctx", xor_perm(lax.axis_size("ctx"), bit))


def swap_fsdp(x, bit):
    return lax.ppermute(x, "fsdp", xor_perm(lax.axis_size("fsdp"), bit))


def side_columns(side, half):
    return pl.ds(pl.multiple_of(side * half, HD), half)


def pack_kernel(plan, key, *refs):
    weights, out, held, sems = refs[:-3], refs[-3], refs[-2], refs[-1]
    copies = []
    for n, (i, row, rows, half, to_row, to_column) in enumerate(plan):
        copies.append(
            pltpu.make_async_copy(
                weights[i].at[row : row + rows, side_columns(key[0], half)],
                held.at[to_row : to_row + rows, to_column : to_column + half],
                sems.at[n],
            )
        )
    for copy in copies:
        copy.start()
    for copy in copies:
        copy.wait()
    last = pltpu.make_async_copy(held, out, sems.at[len(plan)])
    last.start()
    last.wait()


def pack(weights, plan, rows, core):
    columns = max(to_column + half for *_, half, _, to_column in plan)
    dims = (rows, columns)
    return pl.pallas_call(
        functools.partial(pack_kernel, plan),
        in_specs=[smem()] + [anyspace()] * len(weights),
        out_specs=anyspace(),
        out_shape=shape(dims, BF16),
        scratch_shapes=[pltpu.VMEM(dims, BF16), pltpu.SemaphoreType.DMA((len(plan) + 1,))],
        compiler_params=params(56),
        cost_estimate=cost(0, 4 * rows * columns),
        name="pack",
    )(core, *weights)


def unfold_kernel(count, plan, shards, key, mine, twin, *refs):
    total = len(shards)
    outs, held, arrive, leave = refs[:total], refs[total : 2 * total], refs[-2], refs[-1]
    groups, n = [], 0
    for i, shard in enumerate(shards):
        for f in range(count):
            copies = []
            for j, row, rows, half, from_row, from_column in plan:
                if j != i:
                    continue
                for ref, side in ((mine, key[0]), (twin, 1 - key[0])):
                    copies.append(
                        pltpu.make_async_copy(
                            ref.at[f, from_row : from_row + rows, from_column : from_column + half],
                            held[i].at[
                                f * shard + row : f * shard + row + rows, side_columns(side, half)
                            ],
                            arrive.at[n],
                        )
                    )
                    n += 1
            span = slice(f * shard, (f + 1) * shard)
            groups.append(
                (copies, pltpu.make_async_copy(held[i].at[span], outs[i].at[span], leave.at[len(groups)]))
            )
    for copies, _ in groups:
        for copy in copies:
            copy.start()
    for copies, last in groups:
        for copy in copies:
            copy.wait()
        last.start()
    for _, last in groups:
        last.wait()


def unfold_weights(mine, twin, weights, plan, core):
    count = lax.axis_size("fsdp")
    shards = [w.shape[0] for w in weights]
    full = [(w.shape[0] * count, w.shape[1]) for w in weights]
    return pl.pallas_call(
        functools.partial(unfold_kernel, count, plan, shards),
        out_shape=[shape(dims, BF16) for dims in full],
        in_specs=[smem(), anyspace(), anyspace()],
        out_specs=[anyspace()] * len(full),
        scratch_shapes=[pltpu.VMEM(dims, BF16) for dims in full]
        + [
            pltpu.SemaphoreType.DMA((2 * count * len(plan),)),
            pltpu.SemaphoreType.DMA((count * len(full),)),
        ],
        compiler_params=params(60),
        cost_estimate=cost(0, 8 * mine.size),
        name="unfold",
    )(core, mine, twin)


def merge(mine, twin, plan, dims, core):
    half = len(mine)

    def body(key, *refs):
        first, second, outs = refs[:half], refs[half : 2 * half], refs[2 * half :]
        for source, side in ((first, key[0]), (second, 1 - key[0])):
            for i, row, rows, width, n, from_row, from_column, offset, size in plan:
                column = pl.multiple_of(side * width + offset, HD)
                outs[i][row : row + rows, pl.ds(column, size)] = source[n][
                    from_row : from_row + rows, from_column : from_column + size
                ].astype(F32)

    return pl.pallas_call(
        body,
        grid=(1,),
        in_specs=[smem()] + [single(x.shape) for x in (*mine, *twin)],
        out_specs=[single(d) for d in dims],
        out_shape=[shape(d, F32) for d in dims],
        compiler_params=params(56),
        cost_estimate=cost(0, sum(8 * a * b for a, b in dims)),
        name="merge",
    )(core, *mine, *twin)


def fetch_small(vector):
    count = lax.axis_size("fsdp")
    have = {0: vector}
    for bit in bit_list(count):
        for r in list(have):
            have[r ^ bit] = swap_fsdp(have[r], bit)
    stacked = jnp.stack([have[r] for r in range(count)])
    return jnp.take(stacked, lax.axis_index("fsdp") ^ jnp.arange(count), axis=0)


def add_terms(terms):
    total = terms[0].astype(F32)
    for term in terms[1:]:
        total = total + term.astype(F32)
    return total.astype(BF16)


def reduce_steps(keep, send, bits):
    count = lax.axis_size("fsdp")
    ctx_count = lax.axis_size("ctx")
    terms = [keep, (yield "ctx", xor_perm(ctx_count, 1), send)]
    left = count
    for bit in bits:
        left //= 2
        got = yield "fsdp", xor_perm(count, bit), add_terms([t[left:] for t in terms])
        terms = [t[:left] for t in terms] + [got]
    return add_terms([t[0] for t in terms])


def lines():
    return [[g for g in range(lax.axis_size("ctx")) if g % 2 == c] for c in range(2)]


def line_steps(mine, after=None, leave=None):
    ctx_count = lax.axis_size("ctx")
    z = (lax.axis_index("ctx") >> 1) & (LINE - 1)
    stride = 2 * LINE

    def along(pairs):
        return [
            (g * stride + 2 * a + c, g * stride + 2 * b + c)
            for g in range(ctx_count // stride)
            for a, b in pairs
            for c in range(2)
        ]

    if after is not None:
        yield None, None, mine
        mine, _ = lax.optimization_barrier((mine, after[0]))
    got = yield "ctx", along([(0, 1), (3, 2)]), mine
    if leave is not None:
        leave.append(got)
    inner = add_terms([mine, got])
    both = add_terms([inner, (yield "ctx", along([(1, 2), (2, 1)]), inner)])
    outer = yield "ctx", along([(1, 0), (2, 3)]), both
    full = jnp.where((z == 0) | (z == LINE - 1), outer, both)
    bit = stride
    while bit < ctx_count:
        full = add_terms([full, (yield "ctx", xor_perm(ctx_count, bit), full)])
        bit *= 2
    return full, (yield "ctx", xor_perm(ctx_count, 1), full)


def all_steps(keep, send, bits, after, leave):
    return (yield from line_steps((yield from reduce_steps(keep, send, bits)), after, leave))


class Lane:
    def __init__(self):
        self.active = []
        self.done = {}

    def add(self, key, steps):
        self.active.append((key, steps, next(steps)))

    def advance(self, value=None):
        operands = [request[2] for _, _, request in self.active]
        if value is not None and operands:
            value, operands = lax.optimization_barrier((value, operands))
        left = []
        for (key, steps, (axis, pairs, _)), operand in zip(self.active, operands):
            got = None if axis is None else lax.ppermute(operand, axis, pairs)
            try:
                left.append((key, steps, steps.send(got)))
            except StopIteration as stop:
                self.done[key] = stop.value
        self.active = left
        return value

    def drain(self):
        while self.active:
            self.advance()


class Turns:
    def __init__(self):
        self.last = None

    def next(self, value):
        if self.last is not None:
            value, _ = lax.optimization_barrier((value, self.last))
        return value

    def ran(self, value):
        self.last = value
        return value


def grad_kernel(key, a0, a1, k0, k1, s0, s1, *refs):
    keep, send = refs[-2:]
    shard, tile = keep.shape[1], k0.shape[1]
    for n in range(a0.shape[1] // shard):
        left0, left1 = (x[:, n * shard : (n + 1) * shard] for x in (a0, a1))
        span = slice(n * tile, (n + 1) * tile)
        keep[0, :, span] = (dot_tn(left0, k0[...]) + dot_tn(left1, k1[...])).astype(BF16)
        send[0, :, span] = (dot_tn(left0, s0[...]) + dot_tn(left1, s1[...])).astype(BF16)


def shard_order(bits):
    order = [0]
    for bit in reversed(bits):
        order = order + [r | bit for r in order]
    return order


def weight_grad(a, b, shard, tile, first, tiles, bits=None, into=None, place=(0, 0), dims=None):
    count = lax.axis_size("fsdp")
    me = lax.axis_index("fsdp")
    core = lax.axis_index("ctx") & 1
    rows, width = b[0].shape
    across = width // 2 // tile
    chunks = a[0].shape[1] // (count * shard)
    order = jnp.arange(count) if bits is None else me ^ jnp.array(shard_order(bits))
    key = jnp.concatenate([core.reshape(1), order]).astype(jnp.int32)
    dims = dims or (count, shard, chunks * tiles * tile)
    row, column = place
    a_spec = pl.BlockSpec((rows, chunks * shard), lambda t, i, k: (0, k[1 + i]))

    def b_spec(twin):
        return pl.BlockSpec(
            (rows, tile), lambda t, i, k: (0, (1 - k[0] if twin else k[0]) * across + first + t)
        )

    o_spec = pl.BlockSpec((1, shard, chunks * tile), lambda t, i, k: (i, row, column + t))
    extra = list(into or [])
    return pl.pallas_call(
        grad_kernel,
        grid_spec=pltpu.PrefetchScalarGridSpec(
            num_scalar_prefetch=1,
            grid=(tiles, count),
            in_specs=[a_spec, a_spec, b_spec(False), b_spec(False), b_spec(True), b_spec(True)]
            + [anyspace()] * len(extra),
            out_specs=[o_spec, o_spec],
        ),
        out_shape=[shape(dims, BF16)] * 2,
        input_output_aliases={7: 0, 8: 1} if extra else {},
        compiler_params=params(56),
        cost_estimate=cost(
            8 * rows * shard * count * chunks * tiles * tile,
            4 * shard * count * chunks * tiles * tile + 8 * rows * width,
        ),
        name="weight_grad",
    )(key, a[0], a[1], b[0], b[1], b[0], b[1], *extra)


def norm_parts(x):
    centre = x - jnp.mean(x, -1, keepdims=True)
    rstd = lax.rsqrt(jnp.mean(centre * centre, -1, keepdims=True) + EPS)
    return centre * rstd, rstd


def norm_back(x, gain, grad):
    hat, rstd = norm_parts(x)
    scaled = grad * gain
    out = rstd * (
        scaled
        - jnp.mean(scaled, -1, keepdims=True)
        - hat * jnp.mean(scaled * hat, -1, keepdims=True)
    )
    grad_gain = jnp.sum(grad * hat, 0, keepdims=True)
    grad_bias = jnp.sum(grad, 0, keepdims=True)
    return out, grad_gain, grad_bias


GROUP = 8


def qkv_kernel(x_ref, gain, bias, weight, normed, pieces):
    @pl.when(pl.program_id(0) == 0)
    def _():
        hat, _ = norm_parts(x_ref[...].astype(F32))
        normed[...] = (hat * gain[...] + bias[...]).astype(BF16)

    group = dot(normed[...], weight[...]).astype(BF16)
    for copy in range(pieces.shape[0]):
        for h in range(GROUP):
            pieces[copy, h] = group[:, h * HD : (h + 1) * HD]


def qkv_forward(x, gain, bias, weight):
    count = lax.axis_size("ctx")
    width = x.shape[1]
    parts = HEADS // GROUP
    copies = count // HEADS
    normed, pieces = pl.pallas_call(
        qkv_kernel,
        grid=(3 * parts,),
        in_specs=[
            whole(x.shape),
            whole((1, width)),
            whole((1, width)),
            pl.BlockSpec((width, GROUP * HD), lambda t: (0, t)),
        ],
        out_specs=[
            whole((ROWS, width)),
            pl.BlockSpec((copies, GROUP, ROWS, HD), lambda t: (0, t % parts, 0, t // parts)),
        ],
        out_shape=[shape((ROWS, width), BF16), shape((copies, HEADS, ROWS, 3 * HD), BF16)],
        compiler_params=params(56),
        cost_estimate=cost(6 * ROWS * width * width, 8 * width * width),
        name="qkv",
    )(x, gain, bias, weight)
    return normed, pieces.reshape(count, ROWS, 3 * HD)


def gelu(u):
    inner = math.sqrt(2.0 / math.pi) * (u + 0.044715 * u * u * u)
    return 0.5 * u * (1.0 + jnp.tanh(inner))


def gelu_slope(u):
    c = math.sqrt(2.0 / math.pi)
    square = u * u
    t = jnp.tanh(c * (u + 0.044715 * u * square))
    return 0.5 * (1.0 + t) + 0.5 * u * (1.0 - t * t) * (c * (1.0 + 3.0 * 0.044715 * square))


def mlp_kernel(steps, x_ref, w_out, gain, bias, w_in, w_down, pieces, *refs):
    mixed, hidden, normed, up, act, out, total = refs
    step = pl.program_id(0)

    @pl.when(step == 0)
    def _():
        for s in range(HEADS):
            mixed[:, s * HD : (s + 1) * HD] = pieces[s]
        h = x_ref[...].astype(F32) + dot(mixed[...], w_out[...])
        hidden[...] = h
        hat, _ = norm_parts(h)
        normed[...] = (hat * gain[...] + bias[...]).astype(BF16)
        total[...] = h

    u = dot(normed[...], w_in[...])
    up[...] = u.astype(BF16)
    a = gelu(u).astype(BF16)
    act[...] = a
    total[...] += dot(a, w_down[...])

    @pl.when(step == steps - 1)
    def _():
        out[...] = total[...].astype(out.dtype)


def mlp_forward(x, pieces, w_out, gain, bias, w_in, w_down, kind):
    width = x.shape[1]
    ff = w_in.shape[1]
    tile = 1024
    steps = ff // tile
    row = (ROWS, width)
    return pl.pallas_call(
        functools.partial(mlp_kernel, steps),
        grid=(steps,),
        in_specs=[
            whole(row),
            whole(w_out.shape),
            whole((1, width)),
            whole((1, width)),
            pl.BlockSpec((width, tile), lambda j: (0, j)),
            pl.BlockSpec((tile, width), lambda j: (j, 0)),
            whole((HEADS, ROWS, HD)),
        ],
        out_specs=[
            whole(row),
            whole(row),
            whole(row),
            pl.BlockSpec((ROWS, tile), lambda j: (0, j)),
            pl.BlockSpec((ROWS, tile), lambda j: (0, j)),
            whole(row),
        ],
        scratch_shapes=[pltpu.VMEM(row, F32)],
        out_shape=[
            shape(row, BF16),
            shape(row, F32),
            shape(row, BF16),
            shape((ROWS, ff), BF16),
            shape((ROWS, ff), BF16),
            shape(row, kind),
        ],
        compiler_params=params(56),
        cost_estimate=cost(2 * ROWS * width * (width + 2 * ff), 2 * width * (width + 2 * ff)),
        name="mlp",
    )(x, w_out, gain, bias, w_in, w_down, pieces)


def mlp_back_kernel(steps, g_ref, up, w_in, w_down, hidden, gain, w_out, *refs):
    du, grad_low, grad_hidden, grad_gain, grad_bias, pieces, total, low = refs
    step = pl.program_id(0)

    @pl.when(step == 0)
    def _():
        low[...] = g_ref[...].astype(BF16)
        total[...] = jnp.zeros_like(total)

    d_act = dot_nt(low[...], w_down[...])
    d_up = (gelu_slope(up[...].astype(F32)) * d_act).astype(BF16)
    du[...] = d_up
    total[...] += dot_nt(d_up, w_in[...])

    @pl.when(step == steps - 1)
    def _():
        part, g_gain, g_bias = norm_back(hidden[...], gain[...], total[...])
        grad_gain[...] = g_gain
        grad_bias[...] = g_bias
        dh = g_ref[...].astype(F32) + part
        grad_hidden[...] = dh
        hb = dh.astype(BF16)
        grad_low[...] = hb
        mixed = dot_nt(hb, w_out[...]).astype(BF16)
        for s in range(pieces.shape[0]):
            h = s % HEADS
            pieces[s] = mixed[:, h * HD : (h + 1) * HD]


def mlp_backward(grad, up, w_in, w_down, hidden, gain, w_out):
    count = lax.axis_size("ctx")
    width = hidden.shape[1]
    ff = w_in.shape[1]
    tile = 1024
    steps = ff // tile
    row = (ROWS, width)
    return pl.pallas_call(
        functools.partial(mlp_back_kernel, steps),
        grid=(steps,),
        in_specs=[
            whole(row),
            pl.BlockSpec((ROWS, tile), lambda j: (0, j)),
            pl.BlockSpec((width, tile), lambda j: (0, j)),
            pl.BlockSpec((tile, width), lambda j: (j, 0)),
            whole(row),
            whole((1, width)),
            whole(w_out.shape),
        ],
        out_specs=[
            pl.BlockSpec((ROWS, tile), lambda j: (0, j)),
            whole(row),
            whole(row),
            whole((1, width)),
            whole((1, width)),
            whole((count, ROWS, HD)),
        ],
        scratch_shapes=[pltpu.VMEM(row, F32), pltpu.VMEM(row, BF16)],
        out_shape=[
            shape((ROWS, ff), BF16),
            shape(row, BF16),
            shape(row, F32),
            shape((1, width), F32),
            shape((1, width), F32),
            shape((count, ROWS, HD), BF16),
        ],
        compiler_params=params(56),
        cost_estimate=cost(2 * ROWS * width * (width + 2 * ff), 2 * width * (width + 2 * ff)),
        name="mlp_back",
    )(grad, up, w_in, w_down, hidden, gain, w_out)


def qkv_back_kernel(x_ref, gain, grad_hidden, weight, pieces, *refs):
    dqkv, grad_x, grad_low, grad_gain, grad_bias, total = refs
    step = pl.program_id(0)

    @pl.when(step == 0)
    def _():
        total[...] = jnp.zeros_like(total)

    for h in range(GROUP):
        dqkv[:, h * HD : (h + 1) * HD] = pieces[h]
    total[...] += dot_nt(dqkv[...], weight[...])

    @pl.when(step == pl.num_programs(0) - 1)
    def _():
        part, g_gain, g_bias = norm_back(x_ref[...].astype(F32), gain[...], total[...])
        grad_gain[...] = g_gain
        grad_bias[...] = g_bias
        result = grad_hidden[...] + part
        grad_x[...] = result
        grad_low[...] = result.astype(BF16)


def qkv_backward(x, gain, grad_hidden, weight, pieces):
    width = x.shape[1]
    row = (ROWS, width)
    parts = HEADS // GROUP
    wide = GROUP * HD
    return pl.pallas_call(
        qkv_back_kernel,
        grid=(3 * parts,),
        in_specs=[
            whole(row),
            whole((1, width)),
            whole(row),
            pl.BlockSpec((width, wide), lambda t: (0, t)),
            pl.BlockSpec((GROUP, ROWS, HD), lambda t: (t % parts, 0, t // parts)),
        ],
        out_specs=[
            pl.BlockSpec((ROWS, wide), lambda t: (0, t)),
            whole(row),
            whole(row),
            whole((1, width)),
            whole((1, width)),
        ],
        scratch_shapes=[pltpu.VMEM(row, F32)],
        out_shape=[
            shape((ROWS, 3 * width), BF16),
            shape(row, F32),
            shape(row, BF16),
            shape((1, width), F32),
            shape((1, width), F32),
        ],
        compiler_params=params(56),
        cost_estimate=cost(6 * ROWS * width * width, 6 * width * width),
        name="qkv_back",
    )(x, gain, grad_hidden, weight, pieces)


CHUNK = 64


def pick_scores(score_ref, index_ref, base, chunk):
    parts = []
    for r in range(CHUNK // 8):
        at = chunk * CHUNK + r * 8
        rows = pl.ds(pl.multiple_of(at, 8), 8)
        index = index_ref[pl.ds(pl.multiple_of(base + at, 8), 8), :]
        low = index & (HD - 1)
        high = index >> 7
        found = jnp.zeros((8, HD), F32)
        for tile in range(score_ref.shape[1] // HD):
            part = jnp.take_along_axis(
                score_ref[rows, tile * HD : (tile + 1) * HD], low, axis=1, mode="promise_in_bounds"
            )
            found = jnp.where(high == tile, part, found)
        parts.append(found)
    return jnp.concatenate(parts, 0)


def scatter_rows(value_ref, value_base, index_ref, flat_ref, base, dense_ref, group):
    high_count = dense_ref.shape[1] // HD
    row = lax.broadcasted_iota(jnp.int32, (16, HD), 0) & 7
    lane = lax.broadcasted_iota(jnp.int32, (16, HD), 1) >> 5
    masks = [(row == lane + 4 * u).astype(F32).astype(BF16) for u in range(2)]
    place = lax.broadcasted_iota(jnp.int32, (HD, HD), 0).astype(F32).astype(BF16)
    zero, one, none = jnp.zeros((16, HD), BF16), jnp.ones((HD, HD), BF16), jnp.zeros((HD, HD), BF16)
    found = []
    for g in range(2):
        at = group * 16 + g * 8
        value = value_ref[pl.ds(pl.multiple_of(value_base + at, 8), 8), :]
        high = (index_ref[pl.ds(pl.multiple_of(base + at, 8), 8), :] >> 7).astype(F32)
        value = jnp.concatenate([value, value], 0).astype(BF16)
        high = jnp.concatenate([high, high - 1.0], 0).astype(BF16)
        spots = [value * mask for mask in masks]
        bands = []
        for h in range(0, high_count, 2):
            hit = high == jnp.array(h, BF16)
            bands.append(jnp.concatenate([jnp.where(hit, spot, zero) for spot in spots], 1))
        left = jnp.concatenate(bands, 0)
        columns = []
        for u in range(2):
            flat = flat_ref[pl.ds((base + at) // 4 + u, 1), :]
            flat = jnp.broadcast_to(flat, (16, HD)).astype(BF16)
            flat = jnp.concatenate([flat] * (HD // 16), 0)
            columns.append(jnp.where(place == flat, one, none))
        found.append(dot_nt(left, jnp.concatenate(columns, 1)))
    rows = pl.ds(pl.multiple_of(group * 16, 16), 16)
    for h in range(high_count):
        both = [f[h * 8 : (h + 1) * 8, :] for f in found]
        dense_ref[rows, h * HD : (h + 1) * HD] = jnp.concatenate(both, 0).astype(BF16)


def attend_kernel(recall, count, info, rel, buckets, pieces, *refs):
    if recall:
        mem, index, flat = refs[:3]
        refs = refs[3:]
    queries, keys, values, probs, outs = refs[:5]
    refs = refs[5:]
    if recall:
        weights, gap, mixed, bias, scores, dense = refs
    else:
        mixed, bias = refs

    def table(n, carry):
        rows = pl.ds(pl.multiple_of(n * 8, 8), 8)
        bucket = buckets[rows, :]
        part = jnp.full(bucket.shape, NEG, F32)
        for b in range(BUCKETS):
            part = jnp.where(bucket == b, rel[b], part)
        bias[rows, :] = part
        return carry

    lax.fori_loop(0, BLK // 8, table, 0)
    keys[0:WIN, :] = jnp.zeros((WIN, HD), BF16)
    values[0:WIN, :] = jnp.zeros((WIN, HD), BF16)
    for s in range(count):
        queries[s * ROWS : (s + 1) * ROWS, :] = pieces[s, :, :HD]
        for half in range(2):
            row = pl.multiple_of(info[2 * s + half] * BLK + WIN, BLK)
            span = slice(half * BLK, (half + 1) * BLK)
            keys[pl.ds(row, BLK), :] = pieces[s, span, HD : 2 * HD]
            values[pl.ds(row, BLK), :] = pieces[s, span, 2 * HD :]

    def one(s, carry):
        base = pl.multiple_of(s * ROWS, ROWS)
        for half in range(2):
            block = info[2 * s + half]
            row = pl.multiple_of(block * BLK, BLK)
            mine = pl.ds(pl.multiple_of(base + half * BLK, BLK), BLK)
            score = dot_nt(queries[mine, :], keys[pl.ds(row, SPAN), :]) * SCALE + bias[...]
            at = row + lax.broadcasted_iota(jnp.int32, (BLK, 1), 0)
            begin = jnp.zeros((BLK, 1), jnp.int32)
            for d in range(4):
                start = info[2 * count + d]
                begin = jnp.where(at >= start, jnp.maximum(begin, start), begin)
            key_at = row - WIN + lax.broadcasted_iota(jnp.int32, (1, SPAN), 1)
            score = jnp.where(key_at >= begin, score, NEG)
            exps = jnp.exp(score - jnp.max(score, -1, keepdims=True))
            prob = (exps * (1.0 / jnp.sum(exps, -1, keepdims=True))).astype(BF16)
            probs[2 * s + half] = prob
            mixed[mine, :] = dot(prob, values[pl.ds(row, SPAN), :])
        if recall:
            tile = pl.ds(base, ROWS)
            scores[...] = dot_nt(queries[tile, :], mem[:, :HD])

            def choose(chunk, inner):
                found = pick_scores(scores, index, base, chunk) * SCALE
                exps = jnp.exp(found - jnp.max(found, -1, keepdims=True))
                weight = exps * ((HD // TOPK) / jnp.sum(exps, -1, keepdims=True))
                weights[pl.ds(pl.multiple_of(base + chunk * CHUNK, CHUNK), CHUNK), :] = weight
                return inner

            lax.fori_loop(0, ROWS // CHUNK, choose, 0, unroll=4)

            def place(group, inner):
                scatter_rows(weights, base, index, flat, base, dense, group)
                return inner

            lax.fori_loop(0, ROWS // 16, place, 0, unroll=16)
            found = dot(dense[...], mem[:, HD:])
            near = mixed[tile, :]
            gap[tile, :] = found - near
            gate = rel[BUCKETS]
            mixed[tile, :] = gate * found + (1.0 - gate) * near
        return carry

    lax.fori_loop(0, count, one, 0)
    for s in range(count):
        outs[s] = mixed[s * ROWS : (s + 1) * ROWS, :].astype(BF16)


def attend(pieces, info, rel, buckets, memory):
    count = lax.axis_size("ctx")
    total = count * ROWS
    recall = memory is not None
    operands = [info, rel, buckets, pieces]
    outs = [
        shape((total, HD), BF16),
        shape((total + WIN, HD), BF16),
        shape((total + WIN, HD), BF16),
        shape((2 * count, BLK, SPAN), BF16),
        shape((count, ROWS, HD), BF16),
    ]
    scratch = [pltpu.VMEM((total, HD), F32), pltpu.VMEM((BLK, SPAN), F32)]
    if recall:
        operands += list(memory)
        outs += [shape((total, HD), F32), shape((total, HD), F32)]
        rows = memory[0].shape[0]
        scratch += [pltpu.VMEM((ROWS, rows), F32), pltpu.VMEM((ROWS, rows), BF16)]
    result = pl.pallas_call(
        functools.partial(attend_kernel, recall, count),
        grid=(1,),
        in_specs=[smem(), smem()] + [single(x.shape) for x in operands[2:]],
        out_specs=[single(x.shape) for x in outs],
        out_shape=outs,
        scratch_shapes=scratch,
        compiler_params=params(60),
        cost_estimate=cost(45e9 if recall else 12e9, 8e6),
        name="recall_attend" if recall else "local_attend",
    )(*operands)
    return list(result[:4]) + list(result[5:]), result[4]


def attend_back_kernel(recall, count, info, rel, buckets, pieces, *refs):
    queries, keys, values, probs = refs[:4]
    refs = refs[4:]
    if recall:
        weights, gap, mem, index, flat, grad_rel, gate_sum = refs[:7]
        refs = refs[7:]
    else:
        grad_rel, refs = refs[0], refs[1:]
    outs, spread_sum, grads, dq, dk, dv = refs[:6]
    if recall:
        scores, dense, picked, mem_low = refs[6:]
        gate_sum[...] = jnp.zeros_like(gate_sum)
        gate = rel[BUCKETS]

    for s in range(count):
        grads[s * ROWS : (s + 1) * ROWS, :] = pieces[s]
    dk[...] = jnp.zeros_like(dk)
    dv[...] = jnp.zeros_like(dv)
    spread_sum[...] = jnp.zeros_like(spread_sum)

    def one(s, carry):
        base = pl.multiple_of(s * ROWS, ROWS)
        for half in range(2):
            block = info[2 * s + half]
            row = pl.multiple_of(block * BLK, BLK)
            mine = pl.ds(pl.multiple_of(base + half * BLK, BLK), BLK)
            near = pl.ds(row, SPAN)
            grad = grads[mine, :]
            if recall:
                grad = ((1.0 - gate) * grad.astype(F32)).astype(BF16)
            prob_low = probs[2 * s + half]
            prob = prob_low.astype(F32)
            d_prob = dot_nt(grad, values[near, :])
            product = prob * d_prob
            d_score = product - prob * jnp.sum(product, -1, keepdims=True)
            spread_sum[...] += d_score
            low = d_score.astype(BF16)
            dq[mine, :] = dot(low, keys[near, :]) * SCALE
            dk[near, :] += dot_tn(low, queries[mine, :]) * SCALE
            dv[near, :] += dot_tn(prob_low, grad)
        if recall:
            tile = pl.ds(base, ROWS)
            grad = grads[tile, :].astype(F32)
            gate_sum[...] += jnp.sum((grad * gap[tile, :]).reshape(ROWS // 8, 8, HD), 0)
            mem_low[...] = (gate * grad).astype(BF16)
            scores[...] = dot_nt(mem_low[...], mem[:, HD:])

            def choose(chunk, inner):
                found = pick_scores(scores, index, base, chunk)
                rows = pl.ds(pl.multiple_of(base + chunk * CHUNK, CHUNK), CHUNK)
                weight = weights[rows, :]
                product = weight * found
                centre = jnp.sum(product, -1, keepdims=True) * (TOPK / HD)
                local_rows = pl.ds(pl.multiple_of(chunk * CHUNK, CHUNK), CHUNK)
                picked[local_rows, :] = product - weight * centre
                return inner

            lax.fori_loop(0, ROWS // CHUNK, choose, 0, unroll=4)

            def place(group, inner):
                scatter_rows(picked, 0, index, flat, base, dense, group)
                return inner

            lax.fori_loop(0, ROWS // 16, place, 0, unroll=16)
            dq[tile, :] += dot(dense[...], mem[:, :HD]) * SCALE
        return carry

    lax.fori_loop(0, count, one, 0)
    for b in range(BUCKETS):
        part = jnp.sum(jnp.where(buckets[...] == b, spread_sum[...], 0.0), 0, keepdims=True)
        line = part[:, :HD]
        for n in range(1, SPAN // HD):
            line = line + part[:, n * HD : (n + 1) * HD]
        grad_rel[b : b + 1, :] = line
    for s in range(count):
        outs[s, :, :HD] = dq[s * ROWS : (s + 1) * ROWS, :].astype(BF16)
        for half in range(2):
            row = pl.multiple_of(info[2 * s + half] * BLK + WIN, BLK)
            span = slice(half * BLK, (half + 1) * BLK)
            outs[s, span, HD : 2 * HD] = dk[pl.ds(row, BLK), :].astype(BF16)
            outs[s, span, 2 * HD :] = dv[pl.ds(row, BLK), :].astype(BF16)


def attend_back(pieces, info, rel, buckets, saved, memory):
    count = lax.axis_size("ctx")
    total = count * ROWS
    recall = memory is not None
    operands = [info, rel, buckets, pieces, *saved]
    outs = [shape((BUCKETS, HD), F32)]
    scratch = [
        pltpu.VMEM((BLK, SPAN), F32),
        pltpu.VMEM((total, HD), BF16),
        pltpu.VMEM((total, HD), F32),
        pltpu.VMEM((total + WIN, HD), F32),
        pltpu.VMEM((total + WIN, HD), F32),
    ]
    if recall:
        operands += list(memory)
        rows = memory[0].shape[0]
        outs += [shape((8, HD), F32)]
        scratch += [
            pltpu.VMEM((ROWS, rows), F32),
            pltpu.VMEM((ROWS, rows), BF16),
            pltpu.VMEM((ROWS, HD), F32),
            pltpu.VMEM((ROWS, HD), BF16),
        ]
    outs += [shape((count, ROWS, 3 * HD), BF16)]
    result = pl.pallas_call(
        functools.partial(attend_back_kernel, recall, count),
        grid=(1,),
        in_specs=[smem(), smem()] + [single(x.shape) for x in operands[2:]],
        out_specs=[single(x.shape) for x in outs],
        out_shape=outs,
        scratch_shapes=scratch,
        compiler_params=params(60),
        cost_estimate=cost(50e9 if recall else 20e9, 8e6),
        name="recall_back" if recall else "local_back",
    )(*operands)
    return list(result[:-1]), result[-1]


def memory_rows(keys, values, exchange):
    count = lax.axis_size("ctx")

    def pieces(array):
        return [array[:, h * HD : (h + 1) * HD] for h in range(HEADS)]

    both = [jnp.concatenate(pair, 1) for pair in zip(pieces(keys), pieces(values))]
    stacked = jnp.stack(both * (count // HEADS))
    return exchange(stacked).reshape(count * ROWS, 2 * HD)


def memory_index(mem_index, exchange):
    count = lax.axis_size("ctx")
    micro = mem_index.shape[0]
    by_head = jnp.transpose(mem_index, (2, 0, 1, 3)).reshape(HEADS, micro, ROWS * TOPK // HD, HD)
    got = exchange(jnp.concatenate([by_head] * (count // HEADS), 0))
    result = []
    for m in range(micro):
        flat = got[:, m].reshape(-1, HD)
        index = jnp.tile(flat.reshape(count * ROWS, TOPK), (1, HD // TOPK))
        result.append((index, (flat & (HD - 1)).astype(F32)))
    return result


def local(
    inputs,
    block_slots,
    doc_starts,
    mem_index,
    mem_keys,
    mem_values,
    out_grad,
    *weights,
):
    me = lax.axis_index("ctx")
    me_fsdp = lax.axis_index("fsdp")
    count = lax.axis_size("ctx")
    fsdp = lax.axis_size("fsdp")
    micro = inputs.shape[0]
    width = inputs.shape[-1]
    my_head = me & (HEADS - 1)

    layers = [list(weights[:9]), list(weights[9:19])]
    small_of = [[0, 1, 5, 6, 3], [0, 1, 5, 6, 3, 9]]
    small = jnp.concatenate(
        [layers[n][i].reshape(-1) for n in range(2) for i in small_of[n]]
    )
    lengths = [layers[n][i].size for n in range(2) for i in small_of[n]]
    padded = -(-small.shape[0] // HD) * HD
    small = jnp.pad(small, (0, padded - small.shape[0])).reshape(-1, HD)
    gathered = fetch_small(small).reshape(fsdp, -1).astype(F32)
    tables = []
    offset = 0
    for length in lengths:
        tables.append(gathered[:, offset : offset + length])
        offset += length
    norms, rels = [], []
    for n in range(2):
        own = tables[5 * n : 5 * n + 5]
        norms.append([t.reshape(1, width) for t in own[:4]])
        rels.append(own[4].reshape(HEADS, BUCKETS))
    gates = jax.nn.sigmoid(tables[10].reshape(HEADS))
    gate = lax.dynamic_slice_in_dim(gates, my_head, 1, 0)

    buckets = jnp.asarray(window_buckets())
    mine = [
        jnp.concatenate([lax.dynamic_index_in_dim(rels[n], my_head, 0, keepdims=False), gate])
        for n in range(2)
    ]

    ups = bit_list(fsdp)
    downs = ups[::-1]
    tie = lax.optimization_barrier
    core = (me & 1).reshape(1).astype(jnp.int32)
    shard = width // fsdp
    wide = layers[0][7].shape[1]
    chunks = layers[0][8].shape[0] // shard
    half, half_qkv, half_in = width // 2, 3 * width // 2, wide // 2
    quarter = shard // 4
    down = [(n * shard, shard, half, n * half) for n in range(chunks)]
    groups = [
        ([(0, 2)], [(0, 0, shard, half_qkv, 0, 0)], shard),
        (
            [(0, 4), (1, 2), (0, 7), (0, 8)],
            [
                (0, 0, shard, half, 0, 0),
                (1, 0, shard, half_qkv, 0, half),
                (2, 0, shard, half_in, shard, 0),
            ]
            + [(3, row, rows, wide_half, 2 * shard, col) for row, rows, wide_half, col in down],
            3 * shard,
        ),
        (
            [(1, 7), (1, 8), (1, 4)],
            [(0, 0, shard, half_in, 0, 0)]
            + [(1, row, rows, wide_half, shard, col) for row, rows, wide_half, col in down]
            + [(2, n * quarter, quarter, half, 2 * shard, n * half) for n in range(4)],
            2 * shard + quarter,
        ),
    ]
    packed = []
    for ids, plan, count_rows in groups:
        raw = [layers[n][i] for n, i in ids]
        if packed:
            packed[-1], raw = tie((packed[-1], raw))
        packed.append(pack(raw, plan, count_rows, core))
    gathered = [lax.all_gather(p, "fsdp", axis=0, tiled=False) for p in packed]
    full = [{}, {}]

    twins = {}
    turns = Turns()

    def hand_over(g, value):
        value, gathered[g] = tie((value, gathered[g]))
        twins[g] = swap_ctx(gathered[g], 1)
        return value

    def unfold(g):
        ids, plan, _ = groups[g]
        raw = [layers[n][i] for n, i in ids]
        result = unfold_weights(turns.next(gathered[g]), twins[g], raw, plan, core)
        for (n, i), w in zip(ids, result):
            full[n][i] = w
        turns.ran(result[0])


    infos = [
        jnp.concatenate([block_slots[m, 0], doc_starts[m, 0]]).astype(jnp.int32) for m in range(micro)
    ]
    links = Turns()

    def exchange(x):
        return links.ran(lax.all_to_all(links.next(x), "ctx", 0, 0, tiled=False))

    rows = memory_rows(mem_keys[0], mem_values[0], exchange)
    indices = memory_index(mem_index[:, 0], exchange)
    hand_over(0, links.last)
    unfold(0)
    memories = [(rows, *indices[m]) for m in range(micro)]

    state = [inputs[m, 0] for m in range(micro)]
    kept = [None, None]
    projected = [{} for _ in range(micro)]
    for n in range(2):
        gain_in, bias_in, gain_mid, bias_mid = norms[n]
        w = full[n]
        work = [dict(x=state[m]) for m in range(micro)]

        def project(m):
            work[m]["n1"], pieces = qkv_forward(turns.next(work[m]["x"]), gain_in, bias_in, w[2])
            work[m]["pieces"] = exchange(turns.ran(pieces))

        if n == 0:
            for m in range(micro):
                project(m)
        for m in range(micro):
            pieces = turns.next(projected[m]["pieces"] if n else work[m]["pieces"])
            if m == micro - 1:
                pieces = hand_over(1 + n, pieces)
            work[m]["saved"], outs = attend(
                pieces, infos[m], mine[n], buckets, memories[m] if n else None
            )
            work[m]["outs"] = exchange(turns.ran(outs))
        unfold(1 + n)
        for m in range(micro):
            outs = turns.next(work[m]["outs"])
            mixed, hidden, normed_mid, up, act, state[m] = mlp_forward(
                work[m]["x"],
                outs,
                w[4],
                gain_mid,
                bias_mid,
                w[7],
                w[8],
                BF16 if n else F32,
            )
            turns.ran(act)
            work[m].update(mixed=mixed, hidden=hidden, n2=normed_mid, up=up, act=act)
            if n == 0:
                gain, bias = norms[1][:2]
                projected[m]["n1"], pieces = qkv_forward(
                    turns.next(state[m]), gain, bias, full[1][2]
                )
                projected[m]["pieces"] = exchange(turns.ran(pieces))
        if n:
            for m in range(micro):
                work[m]["n1"] = projected[m]["n1"]
        kept[n] = work
    outputs = jnp.stack(state)[:, None]

    lane = Lane()
    smalls = [None, None]

    def pair(source, name):
        return [item[name] for item in source]

    def grad_pair(a, *rest, bits=None, **more):
        both = weight_grad([turns.next(a[0]), *a[1:]], *rest, bits=bits, **more)
        return turns.ran(both)

    def launch(key, bits, *what):
        lane.add(key, reduce_steps(*grad_pair(*what, bits=bits), bits))

    def shard_sum(x):
        return lax.psum_scatter(x, "fsdp", scatter_dimension=0, tiled=False)

    def dense_back(n, m, grad):
        k = kept[n][m]
        w = full[n]
        du, hb, dh, g_gain, g_bias, pieces = mlp_backward(
            turns.next(grad), k["up"], w[7], w[8], k["hidden"], norms[n][2], w[4]
        )
        turns.ran(pieces)
        back[n][m].update(
            du=du, hb=hb, dh=dh, norms=[g_gain, g_bias], pieces=exchange(pieces)
        )

    def heads_back(n, m, pieces):
        item = back[n][m]
        item["extra"], outs = attend_back(
            turns.next(pieces), infos[m], mine[n], buckets, kept[n][m]["saved"],
            memories[m] if n else None,
        )
        item["outs"] = exchange(turns.ran(outs))

    def input_back(n, m, outs):
        k, item = kept[n][m], back[n][m]
        dqkv, dx, dx_low, g_gain, g_bias = qkv_backward(
            k["x"], norms[n][0], item["dh"], full[n][2], turns.next(outs)
        )
        turns.ran(dqkv)
        item.update(dqkv=dqkv, dx=dx, dx_low=dx_low)
        item["norms"] = [g_gain, g_bias] + item["norms"]

    def grad_b(n, top_low):
        ks, items = kept[n], back[n]
        both = grad_pair(
            pair(ks, "n2"), pair(items, "du"), shard, width, 0, half_in // width, dims=dims_b
        )
        return grad_pair(
            pair(ks, "act"), top_low, shard, half, 0, 1, into=both, place=(1, 0), dims=dims_b
        )

    back = [[{} for _ in range(micro)] for _ in range(2)]
    dims_a = (fsdp, shard, 2 * width)
    dims_b = (fsdp, 2 * shard, half_in)
    top = [out_grad[m, 0] for m in range(micro)]
    for m in range(micro):
        dense_back(1, m, top[m])
    keep_b, send_b = grad_b(1, top)
    pieces, send_b = tie((back[1][0]["pieces"], send_b))
    got_b = swap_ctx(send_b, 1)
    heads_back(1, 0, pieces)
    pieces, chip = tie((back[1][1]["pieces"], add_terms([keep_b, turns.next(got_b)])))
    sum_b = shard_sum(chip)
    heads_back(1, 1, pieces)
    both = grad_pair(
        pair(kept[1], "mixed"), pair(back[1], "hb"), shard, half, 0, 1, place=(0, 3), dims=dims_a
    )
    for m in range(micro):
        outs = back[1][m]["outs"]
        if m == 1:
            outs, sum_b = tie((outs, sum_b))
            full_b = lax.psum(sum_b, "ctx", axis_index_groups=lines())
        input_back(1, m, outs)
        dense_back(0, m, back[1][m]["dx"])
    heads_back(0, 0, back[0][0]["pieces"])
    first_in, first_a = [], []
    for key, bits, left, right, tile, after, leave in (
        ("in0", ups, pair(kept[0], "n2"), pair(back[0], "du"), width, None, first_in),
        ("down0", downs, pair(kept[0], "act"), pair(back[1], "dx_low"), half, first_in, None),
    ):
        tiles = right[0].shape[1] // 2 // tile
        both_0 = grad_pair(left, right, shard, tile, 0, tiles, bits=bits)
        lane.add(key, all_steps(*both_0, bits, after, leave))
    heads_back(0, 1, lane.advance(back[0][1]["pieces"]))
    keep_a, send_a = grad_pair(
        pair(kept[1], "n1"), pair(back[1], "dqkv"), shard, half_qkv, 0, 1, into=both, dims=dims_a
    )
    got_a = swap_ctx(send_a, 1)
    input_back(0, 0, lane.advance(back[0][0]["outs"]))
    outs, chip = tie((back[0][1]["outs"], add_terms([keep_a, turns.next(got_a)])))
    sum_a = shard_sum(chip)
    input_back(0, 1, lane.advance(outs))
    n1, dqkv = pair(kept[0], "n1"), pair(back[0], "dqkv")
    launch("low", ups, n1, dqkv, shard, half_qkv // 2, 0, 1)
    launch("high", downs, n1, dqkv, shard, half_qkv // 2, 1, 1)
    launch("out", ups, pair(kept[0], "mixed"), pair(back[0], "hb"), shard, half, 0, 1)
    full_b = turns.next(full_b)
    lane.done["b1"] = full_b, swap_ctx(full_b, 1)
    lane.add("a1", line_steps(sum_a))
    top = pair(back[0], "dx")
    for n in range(2):
        items = back[n]
        share = HEADS / count
        spot = (jnp.arange(HEADS) == my_head).astype(F32) * share
        rel = jnp.sum(sum(item["extra"][0] for item in items), -1)
        parts = [sum(item["norms"][i] for item in items).reshape(fsdp, -1) for i in range(4)]
        parts.append((spot[:, None] * rel[None, :]).reshape(fsdp, -1))
        if n:
            value = sum(jnp.sum(item["extra"][1]) for item in items) * (gate * (1.0 - gate))[0]
            parts.append((spot * value).reshape(fsdp, -1))
        smalls[n] = parts
    dims = [(shard, 3 * width), (shard, width), (shard, wide), (chunks * shard, width)]

    def joined(parts, plan, sizes):
        return merge([p[0] for p in parts], [p[1] for p in parts], plan, sizes, core)

    done = lane.done
    move_in = (0, 0, shard, half_in, 0, 0, 0, 0, half_in)
    move_qkv = (0, 0, shard, half_qkv, 0, 0, 0, 0, half_qkv)
    move_out = (1, 0, shard, half, 0, 0, half_qkv, 0, half)

    def move_down(n, row):
        return [(1, i * shard, shard, half, n, row, i * half, 0, half) for i in range(chunks)]

    grads = [{}, {}]
    while not all(key in lane.done for key in ("low", "high", "out")):
        lane.advance()
    merged = joined([lane.done["b1"]], [move_in] + move_down(0, shard), dims[2:])
    last = jnp.concatenate([lane.done[key] for key in ("low", "high", "out")], 1)
    last, merged = tie((last, merged))
    grads[1][7], grads[1][8] = merged
    lane.add("a00", line_steps(last[: shard // 2], None, first_a))
    lane.add("a01", line_steps(last[shard // 2 :], first_a, None))
    lane.drain()
    parts = [done["in0"], done["down0"]]
    grads[0][7], grads[0][8] = joined(parts, [move_in] + move_down(1, 0), dims[2:])
    grads[1][2], grads[1][4] = joined([done["a1"]], [move_qkv, move_out], dims[:2])
    mid = shard // 2
    moves = [
        (i, n * mid, mid, wide_half, n, 0, col, 0, wide_half)
        for n in range(2)
        for i, wide_half, col in ((0, half_qkv, 0), (1, half, half_qkv))
    ]
    grads[0][2], grads[0][4] = joined([done["a00"], done["a01"]], moves, dims[:2])

    flat = jnp.concatenate(smalls[0] + smalls[1], 1)
    columns = flat.shape[1]
    flat = jnp.pad(flat, ((0, 0), (0, -columns % HD)))
    for bit in bit_list(count):
        flat = flat + swap_ctx(flat, bit)
    for bit in ups:
        flat = flat + swap_fsdp(flat, bit)
    row = lax.dynamic_index_in_dim(flat, me_fsdp, 0, keepdims=False)
    cuts = []
    offset = 0
    for part in smalls[0] + smalls[1]:
        cuts.append(row[offset : offset + part.shape[1]])
        offset += part.shape[1]
    result = []
    for n in range(2):
        own = cuts[5 * n : 5 * n + 5]
        result += [
            own[0],
            own[1],
            grads[n][2],
            own[4].reshape(-1, BUCKETS),
            grads[n][4],
            own[2],
            own[3],
            grads[n][7],
            grads[n][8],
        ]
    result.append(cuts[10])
    return (outputs, jnp.stack(top)[:, None], *result)


def solution(mesh):
    vector, matrix = P("fsdp"), P("fsdp", None)
    rows = P(None, "fsdp", "ctx", None)
    layer = (vector, vector, matrix, matrix, matrix, vector, vector, matrix, matrix)
    table = P(None, "fsdp", None)
    memory = P("fsdp", "ctx", None)
    return jax.shard_map(
        local,
        mesh=mesh,
        in_specs=(rows, table, table, P(None, "fsdp", "ctx", None, None), memory, memory, rows)
        + layer
        + layer
        + (vector,),
        out_specs=(rows, rows) + layer + layer + (vector,),
        check_vma=False,
    )
```
